256 devices in a mesh: tile: 64 (over z, y, core), probe: 4 (over x).
Axes of the slice: x: 4, y: 4, z: 8, core: 2. Of those that a mesh axis runs over, the one named last changes fastest.
Arguments:
- probes: float32 [256, 32, 128], P('tile', 'probe'), may hold values from -6 to 6
- viscosity: float32 [256, 16, 128], P('tile'), may hold values from 0.005 to 0.05
- friction: float32 [256, 128], P('tile'), may hold values from 0.5 to 4
- base_velocity: float32 [256, 2, 128], P('tile'), may hold values from -4 to 4
- obs_tile: int32 [32768, 1], P('tile'), may hold values from 0 to 63; in each aligned block of 512 rows (0 to 511, 512 to 1023, ...) at most 16 rows name the same one
- obs_cell: int32 [32768], P('tile'), may hold values from 0 to 511
- sight_lines: float32 [2, 32768], P(None, 'tile'), may hold values from -1 to 1
- obs_precision: float32 [32768, 512], P('tile'), may hold values from -1 to 32, as said below
- basis: float32 [256, 256, 128], P('probe', 'tile'), may hold values from -0.03125 to 0.03125
Outputs:
- filtered: float32 [256, 32, 128], P('tile', 'probe')
- coefficients: float32 [32, 256], P('probe')
The draws below stay inside these ranges and needn't reach their ends.
Inputs may be any that keep to these rules, and one draw needn't show every extreme that they name: `obs_tile`: within the rows of one owner (aligned blocks of 512 rows) no tile is named by more than 16 rows, and in some block one tile is named by exactly 16 rows. `obs_precision`: each swath's block is symmetric and positive definite.
All inputs are finite; a program needn't handle non-finite values.
Results may differ from the reference program's by a relative error of at most 0.0003.
Values sent between devices are 32-bit elements; how exact they have to be, the bound alone decides.
No kernel may reach another device: no remote copies, remote signals or barrier semaphores. Data moves between devices by JAX's collectives and lax.ppermute only.
A program may use at most 128 MiB of HBM per device.

```python
import math
import jax
import jax.numpy as jnp
import numpy as np
from jax import lax

CX = 4
NY = 128
NZ = 16
K_DEV = 8
NB = 256
OBS_DEV = 512
SWEEPS = 5
NX = 256
K = 32
OBS = 32768
CAP = 16
N_TILE = 64
N_PROBE = 4


def draw_obs_precision(key, part):
    key_spread, key_diag = jax.random.split(key)
    blocks = OBS // OBS_DEV
    spread = jax.random.uniform(key_spread, (blocks, OBS_DEV, OBS_DEV), jnp.float32, -1.0, 1.0) * (4.33 / math.sqrt(OBS_DEV))
    symmetric = 0.5 * (spread + jnp.swapaxes(spread, 1, 2))
    diagonal = jnp.exp(jax.random.uniform(key_diag, (blocks, OBS_DEV), jnp.float32, math.log(4.0), math.log(16.0)))
    identity = jnp.eye(OBS_DEV, dtype=jnp.float32)
    assembled = symmetric * (1.0 - identity) + diagonal[:, :, None] * identity
    return assembled.reshape(OBS, OBS_DEV)


def with_ends(result, stream_key, low, top_value):
    shape = result.shape
    spot = [jax.random.randint(jax.random.fold_in(stream_key, axis), (), 0, shape[axis]) for axis in range(len(shape))]
    result = result.at[tuple(spot)].set(low)
    longest = shape.index(max(shape))
    spot[longest] = (spot[longest] + 1) % shape[longest]
    return result.at[tuple(spot)].set(top_value)


def block_levels(stream_key, dims, cuts, low, top_value):
    gain = 1.0
    for position, blocks in cuts:
        draws = jax.random.uniform(jax.random.fold_in(jax.random.fold_in(stream_key, 6), position), (blocks,), jnp.float32, low / len(cuts), top_value / len(cuts))
        gain = gain * jnp.repeat(jnp.exp(draws), dims[position] // blocks).reshape((-1,) + (1,) * (len(dims) - 1 - position))
    return gain


def shared_out(rng, own, number, rows, amount, top, reach, lean):
    sequence = jax.random.permutation(rng, amount)
    packed, usual = portions_of(amount, rows * top, reach, lean, True), portions_of(amount, rows * top, reach, lean, False)
    places = jnp.arange(amount)

    def named(tallies, offset_by):
        used = int((tallies > 0).sum())
        fixed = max(1, used // 4)
        moved = fixed + (places - fixed + offset_by * (used - fixed)) % max(1, amount - fixed)
        return jnp.zeros((amount,), jnp.int32).at[sequence[jnp.where(places < fixed, places, moved)]].set(jnp.asarray(tallies, jnp.int32))

    tallies = jnp.where(number % 4 == 0, named(packed, number // 4), named(usual, number - number // 4 - 1))
    mixed = jax.random.permutation(jax.random.fold_in(own, 3), amount)
    donor, taker = mixed[0:amount // 2 * 2:2], mixed[1:amount // 2 * 2:2]
    room = jnp.minimum(tallies[donor] - 1, reach - tallies[taker]) // 2
    room = jnp.where((donor == sequence[0]) | (taker == sequence[0]) | (tallies[taker] == 0), 0, jnp.maximum(room, 0))
    moved = jax.random.randint(jax.random.fold_in(own, 4), (amount // 2,), 0, 1 << 20) % (room + 1)
    tallies = tallies.at[donor].add(-moved).at[taker].add(moved)
    items = jnp.searchsorted(jnp.cumsum(tallies), jnp.arange(rows * top), side="right").astype(jnp.int32)
    grid = items.reshape(top, rows).T
    grid = grid[jax.random.permutation(jax.random.fold_in(own, 1), rows)]
    offset_by = jax.random.randint(jax.random.fold_in(own, 2), (rows, 1), 0, top)
    return jnp.take_along_axis(grid, (jnp.arange(top)[None, :] + offset_by) % top, axis=1)


def portions_of(count, total, limit, skew, full):
    portions = [(1 << 20) // math.isqrt(standing ** skew) + 1 for standing in range(1, count + 1)]
    largest = limit if full else min(limit, max(-(-total // count), total * portions[0] // sum(portions)))
    least = 1 if total - largest >= count - 1 else 0
    holding, spare = [largest] + [least] * (count - 1), total - largest - least * (count - 1)
    while spare > 0:
        free = [i for i in range(1, count) if holding[i] < largest] or [i for i in range(1, count) if holding[i] < limit]
        mass, budget = sum([portions[i] for i in free]), spare
        for i in free:
            more = min(limit - holding[i], max(1, budget * portions[i] // mass), spare)
            holding[i] = holding[i] + more
            spare = spare - more
    return np.array(holding)


def gaussian(stream_key, dims, deviation, most, cuts=(), kind=jnp.bfloat16):
    array = deviation * jax.random.normal(stream_key, dims, jnp.float32)
    if cuts:
        array = array * block_levels(stream_key, dims, cuts, -0.22, 0.18)
    return jnp.clip(array, -most, most).astype(kind)


def setup_inputs(seed: int = 0) -> dict:
    splits = jax.random.split(jax.random.key(seed), 10)
    probes = gaussian(splits[0], (NX, K, NY), 1.0, 6.0, ((0, 64), (1, 4)), jnp.float32)
    viscosity = jnp.clip(jnp.exp(math.log(0.05) - 2.3025851 * jax.random.uniform(splits[1], (NX, NZ, NY), jnp.float32) ** block_levels(splits[1], (NX, NZ, NY), ((0, 64),), -0.2, 0.2)), 0.005, 0.05)
    friction = jnp.clip(jnp.exp(math.log(4.0) - 2.0794415 * jax.random.uniform(splits[2], (NX, NY), jnp.float32) ** block_levels(splits[2], (NX, NY), ((0, 64),), -0.2, 0.2)), 0.5, 4.0)
    base_velocity = gaussian(splits[3], (NX, 2, NY), 1.0, 4.0, ((0, 64),), jnp.float32)
    obs_tile_keys = jax.random.split(jax.random.fold_in(splits[4], 1), OBS // OBS_DEV)
    obs_tile_turns = jax.random.permutation(jax.random.fold_in(splits[4], 3), OBS // OBS_DEV)
    obs_tile = jax.vmap(lambda own, number: shared_out(jax.random.fold_in(splits[4], 2), own, number, OBS_DEV, N_TILE, 1, CAP, 2))(obs_tile_keys, obs_tile_turns).reshape((OBS, 1))
    obs_cell = with_ends(jax.random.randint(splits[5], (OBS,), 0, CX * NY), jax.random.fold_in(splits[5], 1), 0, (CX * NY) - 1).astype(jnp.int32)
    sight_lines = jnp.clip(jax.random.uniform(splits[6], (2, OBS), jnp.float32, -1.0, 1.0) * block_levels(splits[6], (2, OBS), ((1, 64),), -0.4, 0.0), -1.0, 1.0)
    obs_precision = draw_obs_precision(jax.random.fold_in(splits[9], 71), 0)
    basis = gaussian(splits[8], (NB, NX, NY), (NX * NY) ** -0.5, 0.03125, ((0, 4), (1, 64)), jnp.float32)
    return {"probes": probes, "viscosity": viscosity, "friction": friction, "base_velocity": base_velocity, "obs_tile": obs_tile, "obs_cell": obs_cell, "sight_lines": sight_lines, "obs_precision": obs_precision, "basis": basis}


aspect_sq = 1024.0
highest = lax.Precision.HIGHEST

def operator_parts(stacked, layers):
    viscous = stacked[:, :layers, :]
    y_padded = jnp.pad(viscous, ((0, 0), (0, 0), (1, 1)))
    centre = viscous[1:-1]
    cells_x = centre.shape[0]
    cells_y = centre.shape[2]
    face_east = 0.5 * (centre + viscous[2:])
    face_west = 0.5 * (centre + viscous[:-2])
    face_north = 0.5 * (centre + y_padded[1:-1, :, 2:])
    face_south = 0.5 * (centre + y_padded[1:-1, :, :-2])
    diagonal_terms = []
    for shift_x in (1, -1):
        for shift_y in (1, -1):
            corner = y_padded[1 + shift_x:1 + shift_x + cells_x, :, 1 + shift_y:1 + shift_y + cells_y]
            diagonal_terms.append(0.375 * shift_x * shift_y * (centre + corner))
    vertical = 0.5 * (centre[:, :-1] + centre[:, 1:])
    empty_row = jnp.zeros_like(centre[:, :1])
    face_up = jnp.concatenate([vertical, empty_row], axis=1)
    face_down = jnp.concatenate([empty_row, vertical], axis=1)
    friction_base = stacked[1:-1, layers]
    basal_term = jnp.concatenate([friction_base[:, None, :], jnp.zeros_like(centre[:, 1:])], axis=1)
    column = aspect_sq * (face_up + face_down) + basal_term
    diag_u = 4.0 * (face_east + face_west) + (face_north + face_south) + column
    diag_v = face_east + face_west + 4.0 * (face_north + face_south) + column
    pivots_main = jnp.stack([diag_u, diag_v], axis=1)
    lower_diag = -aspect_sq * face_down
    upper_diag = -aspect_sq * face_up
    inverses = []
    ratios = []
    for layer_index in range(layers):
        pivot_now = pivots_main[:, :, layer_index]
        if layer_index > 0:
            pivot_now = pivot_now - lower_diag[:, None, layer_index] * ratios[-1]
        inverse = 1.0 / pivot_now
        inverses.append(inverse)
        ratios.append(upper_diag[:, None, layer_index] * inverse)
    horizontal = (face_east[:, None], face_west[:, None], face_north[:, None], face_south[:, None])
    corners = tuple((entry[:, None] for entry in diagonal_terms))
    return (horizontal, corners, lower_diag, inverses, ratios)

def neighbours(extended, stencil_parts):
    horizontal, corners, lower_diag, inverses, ratios = stencil_parts
    face_east, face_west, face_north, face_south = horizontal
    cells_x = extended.shape[0] - 2
    cells_y = extended.shape[4]
    y_padded = jnp.pad(extended, ((0, 0), (0, 0), (0, 0), (0, 0), (1, 1)))

    def shifted(shift_x, shift_y, component):
        return y_padded[1 + shift_x:1 + shift_x + cells_x, :, component, :, 1 + shift_y:1 + shift_y + cells_y]
    along_u = 4.0 * (face_east * shifted(1, 0, 0) + face_west * shifted(-1, 0, 0)) + (face_north * shifted(0, 1, 0) + face_south * shifted(0, -1, 0))
    along_v = face_east * shifted(1, 0, 1) + face_west * shifted(-1, 0, 1) + 4.0 * (face_north * shifted(0, 1, 1) + face_south * shifted(0, -1, 1))
    offsets = ((1, 1), (1, -1), (-1, 1), (-1, -1))
    cross_u = corners[0] * shifted(offsets[0][0], offsets[0][1], 1)
    cross_v = corners[0] * shifted(offsets[0][0], offsets[0][1], 0)
    for which in range(1, 4):
        cross_u = cross_u + corners[which] * shifted(offsets[which][0], offsets[which][1], 1)
        cross_v = cross_v + corners[which] * shifted(offsets[which][0], offsets[which][1], 0)
    return jnp.stack([along_u + cross_u, along_v + cross_v], axis=2)

def column_solve(right_side, load_layer, loading, stencil_parts):
    horizontal, corners, lower_diag, inverses, ratios = stencil_parts
    layers = len(inverses)
    forward = []
    for layer_index in range(layers):
        if right_side is None:
            current = loading if layer_index == load_layer else jnp.zeros_like(loading)
        else:
            current = right_side[:, :, :, layer_index]
            if layer_index == load_layer:
                current = current + loading
        if layer_index > 0:
            current = current - lower_diag[:, None, None, layer_index] * forward[-1]
        forward.append(current * inverses[layer_index][:, None])
    solved = [forward[-1]]
    for layer_index in range(layers - 2, -1, -1):
        solved.insert(0, forward[layer_index] - ratios[layer_index][:, None] * solved[0])
    return jnp.stack(solved, axis=3)

def relax(loading, load_layer, stencil_parts):
    velocity = column_solve(None, load_layer, loading, stencil_parts)
    for sweep_index in range(SWEEPS - 1):
        extended = jnp.pad(velocity, ((1, 1), (0, 0), (0, 0), (0, 0), (0, 0)))
        velocity = column_solve(neighbours(extended, stencil_parts), load_layer, loading, stencil_parts)
    return velocity

def reference(probes, viscosity, friction, base_velocity, obs_tile, obs_cell, sight_lines, obs_precision, basis):
    stacked = jnp.concatenate([viscosity, friction[:, None, :], base_velocity], axis=1)
    padded = jnp.pad(stacked, ((1, 1), (0, 0), (0, 0)))
    stencil_parts = operator_parts(padded, NZ)
    basal_gain = -(friction[:, None, None, :] * base_velocity[:, None, :, :])
    cell_index = (obs_tile[:, 0] * (CX * NY) + obs_cell).astype(jnp.int32)
    precision_blocks = obs_precision.reshape(N_TILE, OBS_DEV, OBS_DEV)
    sight_rows = jnp.transpose(sight_lines)

    def one_group(probe_group):
        loading = basal_gain * probe_group[:, :, None, :]
        velocity_state = relax(loading, 0, stencil_parts)
        surface = velocity_state[:, :, :, NZ - 1, :]
        surface_cells = jnp.transpose(surface, (0, 3, 1, 2)).reshape(NX * NY, K_DEV, 2)
        picked = surface_cells[cell_index]
        predicted = sight_rows[:, 0:1] * picked[:, :, 0] + sight_rows[:, 1:2] * picked[:, :, 1]
        weighted = jnp.einsum('sij,sjk->sik', precision_blocks, predicted.reshape(N_TILE, OBS_DEV, K_DEV), precision=highest)
        weighted = weighted.reshape(N_TILE * OBS_DEV, K_DEV)
        row_loads = weighted[:, :, None] * sight_rows[:, None, :]
        top_sum = jax.ops.segment_sum(row_loads, cell_index, num_segments=NX * NY)
        top_load = jnp.transpose(top_sum.reshape(NX, NY, K_DEV, 2), (0, 2, 3, 1))
        adjoint = relax(top_load, NZ - 1, stencil_parts)
        return jnp.sum(basal_gain * adjoint[:, :, :, 0, :], axis=2)
    groups = jnp.transpose(probes.reshape(NX, N_PROBE, K_DEV, NY), (1, 0, 2, 3))
    hessian_groups = lax.map(one_group, groups)
    hessian = jnp.transpose(hessian_groups, (1, 0, 2, 3)).reshape(NX, N_PROBE * K_DEV, NY)
    gram = jnp.einsum('bxy,cxy->bc', basis, basis, precision=highest)
    moments = jnp.einsum('bxy,xky->bk', basis, hessian, precision=highest)
    factor = jnp.linalg.cholesky(gram)
    coeffs = jax.scipy.linalg.cho_solve((factor, True), moments)
    filtered = hessian - jnp.einsum('bxy,bk->xky', basis, coeffs, precision=highest)
    return (filtered, jnp.transpose(coeffs))
```

```python
import functools

import jax
import jax.numpy as jnp
from jax import lax
from jax.experimental import pallas as pl
from jax.experimental.pallas import tpu as pltpu
from jax.sharding import PartitionSpec as P

SWEEPS = 5
CX = 4
NY = 128
NZ = 16
KD = 8
CAP = 16
TILES = 64
ROWS = CX * 3
ASPECT = 1024.0
N_COEF = 13
F_E, F_W, A_N, A_S, C_PP, C_MP, C_PM, C_MM, LOW, INV_U, INV_V, Q_U, Q_V = range(N_COEF)
BLOCK = 64
f32 = jnp.float32
bf16 = jnp.bfloat16
PARAMS = pltpu.CompilerParams(vmem_limit_bytes=32 * 2**20)
VM = pl.BlockSpec(memory_space=pltpu.VMEM)
SM = pl.BlockSpec(memory_space=pltpu.SMEM)

NN = (((1,), (0,)), ((), ()))
NT = (((1,), (1,)), ((), ()))


def call(kernel, out_shape, args, scratch=(), scalars=0, flops=0, moved=0, aliases=None):
    single = not isinstance(out_shape, (list, tuple))
    shapes = [out_shape] if single else list(out_shape)
    out = pl.pallas_call(
        kernel,
        out_shape=shapes,
        in_specs=[SM] * scalars + [VM] * (len(args) - scalars),
        out_specs=[VM] * len(shapes),
        scratch_shapes=list(scratch),
        compiler_params=PARAMS,
        input_output_aliases=aliases or {},
        cost_estimate=pl.CostEstimate(flops=flops, bytes_accessed=moved, transcendentals=0),
    )(*args)
    return out[0] if single else out


def sds(shape, dtype=f32):
    return jax.ShapeDtypeStruct(shape, dtype)


def dot(a, b, dims):
    return lax.dot_general(a, b, dims, preferred_element_type=f32)


def split2(x):
    high = x.astype(bf16)
    return high, (x - high.astype(f32)).astype(bf16)


def split3(x):
    high = x.astype(bf16)
    rest = x - high.astype(f32)
    middle = rest.astype(bf16)
    return high, middle, (rest - middle.astype(f32)).astype(bf16)


def dot3(a, b, dims):
    a_high, a_low = a
    b_high, b_low = b
    return dot(a_high, b_high, dims) + (dot(a_high, b_low, dims) + dot(a_low, b_high, dims))


def iota(shape, axis):
    return lax.broadcasted_iota(jnp.int32, shape, axis)


def meta_kernel(tile_ref, cell_ref, sight_ref, payload_ref, rank_ref):
    rows = tile_ref.shape[1]
    one_hot = (iota((TILES, rows), 0) == tile_ref[...]).astype(f32)
    before = (iota((rows, rows), 0) < iota((rows, rows), 1)).astype(f32).astype(bf16)
    one_hot_b = one_hot.astype(bf16)
    earlier = dot(one_hot_b, before, NN)
    rank = jnp.sum(one_hot * earlier, axis=0, keepdims=True).astype(jnp.int32)
    rank_ref[...] = rank
    chosen = (iota((CAP, rows), 0) == rank).astype(f32)
    values = jnp.concatenate(
        [
            chosen * cell_ref[...].astype(f32),
            chosen * sight_ref[0:1, :],
            chosen * sight_ref[1:2, :],
            jnp.zeros((128 - 3 * CAP, rows), f32),
        ],
        axis=0,
    )
    parts = [dot(one_hot_b, part, NT) for part in split3(values)]
    payload_ref[...] = parts[0] + (parts[1] + parts[2])


def build_coefs(visc, fric, coef, upper):
    lane = iota((NZ, NY), 1)
    layer = iota((NZ, NY), 0)

    def row(i, carry):
        centre = visc[i]
        east = visc[i + 1]
        west = visc[i - 1]

        def from_south(x):
            return pltpu.roll(x, 1, 1)

        def from_north(x):
            return pltpu.roll(x, NY - 1, 1)

        south_centre = jnp.where(lane == 0, 0.0, from_south(centre))
        north_centre = jnp.where(lane == NY - 1, 0.0, from_north(centre))
        face_e = 0.5 * (centre + east)
        face_w = 0.5 * (centre + west)
        face_n = 0.5 * (centre + north_centre)
        face_s = 0.5 * (centre + south_centre)
        coef[F_E, i - 1] = face_e
        coef[F_W, i - 1] = face_w
        coef[A_N, i - 1] = jnp.where(lane == 0, 0.0, face_s)
        coef[A_S, i - 1] = jnp.where(lane == NY - 1, 0.0, face_n)
        coef[C_PP, i - 1] = jnp.where(lane == 0, 0.0, 0.375 * (south_centre + east))
        coef[C_MP, i - 1] = jnp.where(lane == 0, 0.0, -0.375 * (south_centre + west))
        coef[C_PM, i - 1] = jnp.where(lane == NY - 1, 0.0, -0.375 * (north_centre + east))
        coef[C_MM, i - 1] = jnp.where(lane == NY - 1, 0.0, 0.375 * (north_centre + west))
        above = pltpu.roll(centre, NZ - 1, 0)
        up = jnp.where(layer == NZ - 1, 0.0, ASPECT * 0.5 * (centre + above))
        down = jnp.where(layer == 0, 0.0, pltpu.roll(up, 1, 0))
        coef[LOW, i - 1] = down
        upper[i - 1] = up
        column = (up + down) + jnp.where(layer == 0, fric[i - 1], 0.0)
        coef[INV_U, i - 1] = 4.0 * (face_e + face_w) + (face_n + face_s) + column
        coef[INV_V, i - 1] = face_e + face_w + 4.0 * (face_n + face_s) + column
        return carry

    lax.fori_loop(1, ROWS + 1, row, 0)
    inside = visc[pl.ds(1, ROWS), 0, :] > 0.0
    ratio_u = ratio_v = None
    for layer_index in range(NZ):
        pivot_u = coef[INV_U, :, layer_index, :]
        pivot_v = coef[INV_V, :, layer_index, :]
        if layer_index > 0:
            low = coef[LOW, :, layer_index, :]
            pivot_u = pivot_u - low * ratio_u
            pivot_v = pivot_v - low * ratio_v
        inverse_u = jnp.where(inside, 1.0 / pivot_u, 0.0)
        inverse_v = jnp.where(inside, 1.0 / pivot_v, 0.0)
        up = upper[:, layer_index, :]
        ratio_u = up * inverse_u
        ratio_v = up * inverse_v
        coef[INV_U, :, layer_index, :] = inverse_u
        coef[INV_V, :, layer_index, :] = inverse_v
        coef[Q_U, :, layer_index, :] = ratio_u
        coef[Q_V, :, layer_index, :] = ratio_v


def run_sweeps(coef, load, fields, load_layer, finish):
    far = NZ - 1 if load_layer == 0 else 0

    def take(which, i, layer_index):
        return jnp.broadcast_to(coef[which, i, layer_index : layer_index + 1, :], (KD, NY))

    def solve(i, right_u, right_v, last):
        forward_u, forward_v = [], []
        for k in range(NZ):
            u, v = right_u(k), right_v(k)
            if k == load_layer:
                u = load[i, 0] if u is None else u + load[i, 0]
                v = load[i, 1] if v is None else v + load[i, 1]
            if k > 0 and forward_u[-1] is not None:
                low = take(LOW, i, k)
                below_u, below_v = low * forward_u[-1], low * forward_v[-1]
                u = below_u if u is None else u + below_u
                v = below_v if v is None else v + below_v
            forward_u.append(None if u is None else u * take(INV_U, i, k))
            forward_v.append(None if v is None else v * take(INV_V, i, k))
        solved_u, solved_v = [None] * NZ, [None] * NZ
        solved_u[-1], solved_v[-1] = forward_u[-1], forward_v[-1]
        if not (last and far == NZ - 1):
            for k in range(NZ - 2, -1, -1):
                u = take(Q_U, i, k) * solved_u[k + 1]
                v = take(Q_V, i, k) * solved_v[k + 1]
                solved_u[k] = u if forward_u[k] is None else forward_u[k] + u
                solved_v[k] = v if forward_v[k] is None else forward_v[k] + v
        return solved_u, solved_v

    for sweep in range(SWEEPS):
        source, target = fields[(sweep + 1) % 2], fields[sweep % 2]
        last = sweep == SWEEPS - 1

        def row(i, carry, sweep=sweep, source=source, target=target, last=last):
            if sweep == 0:
                nothing = lambda k: None
                solved_u, solved_v = solve(i, nothing, nothing, last)
            else:

                def sides(component, k, along):
                    other = 1 - component
                    mine, east, west = (source[i + d, component, k] for d in (0, 1, -1))
                    cross_e, cross_w = (source[i + d, other, k] for d in (1, -1))
                    direct = take(F_E, i, k) * east + take(F_W, i, k) * west
                    if along:
                        direct = 4.0 * direct
                        scaled = mine
                    else:
                        scaled = 4.0 * mine
                    north = take(A_N, i, k) * scaled + (
                        take(C_PP, i, k) * cross_e + take(C_MP, i, k) * cross_w
                    )
                    south = take(A_S, i, k) * scaled + (
                        take(C_PM, i, k) * cross_e + take(C_MM, i, k) * cross_w
                    )
                    return direct + (pltpu.roll(north, NY - 1, 1) + pltpu.roll(south, 1, 1))

                solved_u, solved_v = solve(
                    i,
                    lambda k: sides(0, k, True),
                    lambda k: sides(1, k, False),
                    last,
                )
            if last:
                finish(i - CX, solved_u[far], solved_v[far])
            else:
                for k in range(NZ):
                    target[i, 0, k] = solved_u[k]
                    target[i, 1, k] = solved_v[k]
            return carry

        lax.fori_loop(sweep, ROWS - sweep, row, 0)


V_AT, P_AT, B_AT, F_AT, PACK = 0, CX * NZ, CX * (NZ + KD), CX * (NZ + KD + 2), 112


def state_kernel(
    own, left, right, far_left, far_right, surface, coef, gain, visc, upper, fric, load, field_a, field_b
):
    visc[0] = far_left[...]
    visc[ROWS + 1] = far_right[...]
    for part, packed in enumerate((left, own, right)):
        for x in range(CX):
            i = part * CX + x
            visc[i + 1] = packed[V_AT + x * NZ : V_AT + (x + 1) * NZ, :]
            friction = packed[F_AT + x : F_AT + x + 1, :]
            fric[i] = friction
            probes = packed[P_AT + x * KD : P_AT + (x + 1) * KD, :]
            for m in range(2):
                basal = -(friction * packed[B_AT + 2 * x + m : B_AT + 2 * x + m + 1, :])
                if part == 1:
                    gain[m, x : x + 1, :] = basal
                load[i, m] = basal * probes
    build_coefs(visc, fric, coef, upper)

    def finish(x, u, v):
        surface[0, x] = u
        surface[1, x] = v

    run_sweeps(coef, load, (field_a, field_b), 0, finish)


def adjoint_kernel(
    own, left, right, coef, gain, panel_high, panel_low, hessian, moments, load, field_a, field_b
):
    for part, packed in enumerate((left, own, right)):
        for x in range(CX):
            for m in range(2):
                load[part * CX + x, m] = packed[m * KD : (m + 1) * KD, x * NY : (x + 1) * NY]

    def finish(x, u, v):
        hessian[x] = gain[0, pl.ds(x, 1), :] * u + gain[1, pl.ds(x, 1), :] * v

    run_sweeps(coef, load, (field_a, field_b), NZ - 1, finish)
    whole = jnp.concatenate([hessian[x] for x in range(CX)], axis=1)
    moments[...] = dot3(split2(whole), (panel_high[...], panel_low[...]), NT)


def gram_kernel(me_ref, own, near, across, back, panel_high, panel_low, part):
    me = me_ref[0]
    count = own.shape[0] // CX
    mine = None
    for shift, block in enumerate((own, near, across, back)):
        source = lax.rem(me - shift + 4, 4)
        flat = jnp.concatenate(
            [block[pl.ds(x, count, stride=CX), :] for x in range(CX)], axis=1
        )
        high, low = split2(flat)
        if shift == 0:
            mine = (high, low)
        at = pl.ds(pl.multiple_of(source * count, count), count)
        panel_high[at, :] = high
        panel_low[at, :] = low
    part[...] = dot3(mine, (panel_high[...], panel_low[...]), NT)


def invert_block(block):
    size = block.shape[0]
    row_of = iota(block.shape, 0)
    lane_of = iota(block.shape, 1)
    for k in range(size):
        column = jnp.broadcast_to(block[:, k : k + 1], block.shape)
        inverse = 1.0 / jnp.broadcast_to(column[k : k + 1, :], (1, size))
        pivot_row = jnp.where(lane_of[0:1, :] == k, 1.0, block[k : k + 1, :]) * inverse
        column = jnp.where(row_of == k, -1.0, column)
        block = jnp.where((row_of == k) | (lane_of == k), 0.0, block) - column * pivot_row
    return block


def dot_f32(a, b):
    a1, a2, a3 = split3(a)
    b1, b2, b3 = split3(b)
    small = dot(a1, b3, NN) + dot(a3, b1, NN) + dot(a2, b2, NN)
    return dot(a1, b1, NN) + ((dot(a1, b2, NN) + dot(a2, b1, NN)) + small)


def eliminate(matrix, number):
    size = matrix.shape[0]
    at = slice(number * BLOCK, (number + 1) * BLOCK)
    inverse = invert_block(matrix[at, at])
    panel = matrix[at, :]
    columns = matrix[:, at]
    lanes = iota((BLOCK, size), 1)
    own_lanes = (lanes >= number * BLOCK) & (lanes < (number + 1) * BLOCK)
    identity = (iota((BLOCK, size), 0) + number * BLOCK == lanes).astype(f32)
    rows = dot_f32(inverse, jnp.where(own_lanes, identity, panel))
    rest = matrix[...]
    all_lanes = iota((size, size), 1)
    inside = (all_lanes >= number * BLOCK) & (all_lanes < (number + 1) * BLOCK)
    matrix[...] = jnp.where(inside, 0.0, rest) - dot_f32(columns, rows)
    matrix[at, :] = rows


def first_kernel(me_ref, own, near, across, back, matrix):
    me = me_ref[0]
    count = own.shape[0]
    for shift, block in enumerate((own, near, across, back)):
        source = lax.rem(me - shift + 4, 4)
        matrix[pl.ds(pl.multiple_of(source * count, count), count), :] = block[...]
    eliminate(matrix, 0)


def next_kernel(number, before, matrix):
    matrix[...] = before[...]
    eliminate(matrix, number)


def slot_rows(meta):
    wide = jnp.concatenate([meta[...], jnp.zeros((128 - TILES, 128), f32)], axis=0)
    turned = jnp.transpose(wide)
    half = CAP // 2

    def paired(at):
        return turned[at : at + half] + pltpu.roll(turned[at + half : at + CAP], TILES, 1)

    return paired(0), paired(CAP), paired(2 * CAP)


def slot_one_hot(cells):
    index = cells.astype(jnp.int32)
    at = iota((CX * NY, 128), 0)
    return jnp.concatenate(
        [(at == index[j : j + 1, :]).astype(f32).astype(bf16) for j in range(CAP // 2)], axis=1
    )


def gather_kernel(meta, surface, gram_part, payload):
    cells, sight_u, sight_v = slot_rows(meta)
    one_hot = slot_one_hot(cells)
    both = jnp.concatenate(
        [jnp.concatenate([surface[m, x] for x in range(CX)], axis=1) for m in range(2)], axis=0
    )
    picked = dot(jnp.concatenate(split3(both), axis=0), one_hot, NN)
    n = 2 * KD
    picked = picked[0:n] + (picked[n : 2 * n] + picked[2 * n : 3 * n])
    chunks = []
    for j in range(CAP // 2):
        at = slice(j * 128, (j + 1) * 128)
        chunks.append(
            sight_u[j : j + 1, :] * picked[0:KD, at] + sight_v[j : j + 1, :] * picked[KD:n, at]
        )
    chunks.append(jnp.zeros((128 - TILES, 128), f32))
    turned = jnp.transpose(jnp.concatenate(chunks, axis=0))
    payload[pl.ds(0, TILES, stride=4), :] = turned[0:TILES] + pltpu.roll(turned[TILES:], TILES, 1)
    payload[pl.ds(1, TILES, stride=4), :] = gram_part[:, 0:128]
    payload[pl.ds(2, TILES, stride=4), :] = gram_part[:, 128:256]
    payload[pl.ds(3, TILES, stride=4), :] = jnp.zeros((TILES, 128), f32)


def precision_kernel(arrived, tile_ref, rank_ref, precision, payload):
    rows = tile_ref.shape[1]
    one_hot = (iota((128, rows), 0) == tile_ref[...]).astype(f32).astype(bf16)
    rank = rank_ref[...]
    mine = arrived[pl.ds(0, TILES, stride=4), :]
    turned = jnp.transpose(jnp.concatenate([mine, jnp.zeros((128 - TILES, 128), f32)], axis=0))
    spread = [dot(part, one_hot, NN) for part in split3(turned)]
    spread = spread[0] + (spread[1] + spread[2])
    predicted = jnp.zeros((KD, rows), f32)
    for s in range(CAP):
        predicted = predicted + jnp.where(rank == s, spread[s * KD : (s + 1) * KD], 0.0)
    weighted = dot3(split2(predicted), split2(precision[...]), NN)
    slots = jnp.concatenate([jnp.where(rank == s, weighted, 0.0) for s in range(CAP)], axis=0)
    sent = [dot(one_hot, part, NT) for part in split3(slots)]
    sent = sent[0] + (sent[1] + sent[2])
    payload[pl.ds(0, TILES, stride=4), :] = sent[0:TILES]
    for k in (1, 2):
        total = jnp.sum(arrived[pl.ds(k, TILES, stride=4), :], axis=0, keepdims=True)
        payload[pl.ds(k, TILES, stride=4), :] = jnp.broadcast_to(total, (TILES, 128))
    payload[pl.ds(3, TILES, stride=4), :] = jnp.zeros((TILES, 128), f32)


def scatter_kernel(returned, meta, top, gram_rows):
    cells, sight_u, sight_v = slot_rows(meta)
    one_hot = slot_one_hot(cells)
    mine = returned[pl.ds(0, TILES, stride=4), :]
    turned = jnp.transpose(jnp.concatenate([mine, pltpu.roll(mine, TILES, 1)], axis=0))
    loads = []
    for sight in (sight_u, sight_v):
        loads.append(
            jnp.concatenate(
                [turned[j * KD : (j + 1) * KD] * sight[j : j + 1, :] for j in range(CAP // 2)],
                axis=1,
            )
        )
    parts = dot(jnp.concatenate(split3(jnp.concatenate(loads, axis=0)), axis=0), one_hot, NT)
    n = 2 * KD
    top[...] = parts[0:n] + (parts[n : 2 * n] + parts[2 * n : 3 * n])
    gram_rows[:, 0:128] = returned[pl.ds(1, TILES, stride=4), :]
    gram_rows[:, 128:256] = returned[pl.ds(2, TILES, stride=4), :]


def final_kernel(moments, inverse, panel_high, panel_low, hessian, filtered, coefficients):
    solved = dot_f32(moments[...], inverse[...])
    coefficients[...] = solved
    removed = dot3(split2(solved), (panel_high[...], panel_low[...]), NN)
    for x in range(CX):
        filtered[x] = hessian[x] - removed[:, x * NY : (x + 1) * NY]


def along(value, axis, shift):
    count = lax.axis_size(axis)
    return lax.ppermute(
        value, axis, [(i, i + shift) for i in range(count) if 0 <= i + shift < count]
    )


def around(value, axis, shift):
    count = lax.axis_size(axis)
    return lax.ppermute(value, axis, [(i, (i + shift) % count) for i in range(count)])


def per_device(
    probes, viscosity, friction, base_velocity, obs_tile, obs_cell, sight_lines, obs_precision, basis
):
    cells = CX * NY
    me = lax.axis_index("probe").astype(jnp.int32).reshape(1)
    packed = jnp.concatenate(
        [
            viscosity.reshape(CX * NZ, NY),
            probes.reshape(CX * KD, NY),
            base_velocity.reshape(CX * 2, NY),
            friction,
            jnp.zeros((PACK - F_AT - CX, NY), f32),
        ],
        axis=0,
    )
    left = along(packed, "tile", 1)
    right = along(packed, "tile", -1)
    far_left = along(viscosity[CX - 1], "tile", 2)
    far_right = along(viscosity[0], "tile", -2)

    tile_row = obs_tile.reshape(1, -1)
    rows = tile_row.shape[1]
    asked, rank = call(
        meta_kernel,
        [sds((TILES, 128)), sds((1, rows), jnp.int32)],
        [tile_row, obs_cell.reshape(1, -1), sight_lines],
        flops=2 * 64 * 512 * 1000,
        moved=10000,
    )
    meta = lax.all_to_all(asked, "tile", split_axis=0, concat_axis=0, tiled=True)

    own_basis = basis.reshape(-1, NY)
    others = [around(own_basis, "probe", d) for d in (1, 2, 3)]

    field = pltpu.VMEM((ROWS, 2, NZ, KD, NY), f32)
    load = pltpu.VMEM((ROWS, 2, KD, NY), f32)
    surface, coef, gain = call(
        state_kernel,
        [sds((2, CX, KD, NY)), sds((N_COEF, ROWS, NZ, NY)), sds((2, CX, NY))],
        [packed, left, right, far_left, far_right],
        scratch=[
            pltpu.VMEM((ROWS + 2, NZ, NY), f32),
            pltpu.VMEM((ROWS, NZ, NY), f32),
            pltpu.VMEM((ROWS, 1, NY), f32),
            load,
            field,
            field,
        ],
        flops=40 * 16 * 44 * 1024,
        moved=2000000,
    )
    n_basis = 4 * basis.shape[0]
    panel_high, panel_low, gram_part = call(
        gram_kernel,
        [sds((n_basis, cells), bf16), sds((n_basis, cells), bf16), sds((TILES, n_basis))],
        [me, own_basis, *others],
        scalars=1,
        flops=6 * 64 * 512 * 256,
        moved=1500000,
    )
    payload = call(
        gather_kernel,
        sds((TILES * 4, 128)),
        [meta, surface, gram_part],
        flops=2 * 48 * 512 * 1024,
        moved=300000,
    )

    def exchange(value):
        return lax.all_to_all(
            value.reshape(TILES, 4, 128), "tile", split_axis=0, concat_axis=0, tiled=True
        ).reshape(TILES * 4, 128)

    arrived = exchange(payload)
    outgoing = call(
        precision_kernel,
        sds((TILES * 4, 128)),
        [arrived, tile_row, rank, obs_precision],
        flops=2 * 512 * 512 * 64,
        moved=1500000,
    )
    returned = exchange(outgoing)
    top, gram_rows = call(
        scatter_kernel,
        [sds((2 * KD, cells)), sds((TILES, n_basis))],
        [returned, meta],
        flops=2 * 48 * 512 * 1024,
        moved=300000,
    )
    top_left = along(top, "tile", 1)
    top_right = along(top, "tile", -1)
    quarters = [around(gram_rows, "probe", d) for d in (1, 2, 3)]
    hessian, moments = call(
        adjoint_kernel,
        [sds((CX, KD, NY)), sds((KD, n_basis))],
        [top, top_left, top_right, coef, gain, panel_high, panel_low],
        scratch=[load, field, field],
        flops=40 * 16 * 44 * 1024,
        moved=2000000,
    )
    matrix = call(
        first_kernel,
        sds((n_basis, n_basis)),
        [me, gram_rows, *quarters],
        scalars=1,
        flops=12 * 64 * 256 * 256,
        moved=500000,
    )
    for number in range(1, n_basis // BLOCK):
        matrix = call(
            functools.partial(next_kernel, number),
            sds((n_basis, n_basis)),
            [matrix],
            flops=12 * 64 * 256 * 256,
            moved=500000,
        )
    step = 1
    while step < TILES:
        moments = moments + lax.ppermute(moments, "tile", [(i, i ^ step) for i in range(TILES)])
        step *= 2
    filtered, coefficients = call(
        final_kernel,
        [sds((CX, KD, NY)), sds((KD, n_basis))],
        [moments, matrix, panel_high, panel_low, hessian],
        flops=12 * 8 * 256 * 512,
        moved=800000,
    )
    return filtered, coefficients


def solution(mesh):
    in_specs = (
        P("tile", "probe", None),
        P("tile", None, None),
        P("tile", None),
        P("tile", None, None),
        P("tile", None),
        P("tile"),
        P(None, "tile"),
        P("tile", None),
        P("probe", "tile", None),
    )
    out_specs = (P("tile", "probe", None), P("probe", None))
    return jax.shard_map(
        per_device, mesh=mesh, in_specs=in_specs, out_specs=out_specs, check_vma=False
    )
```

```python
import functools

import jax
import jax.numpy as jnp
from jax import lax
from jax.experimental import pallas as pl
from jax.experimental.pallas import tpu as pltpu
from jax.sharding import PartitionSpec as P

SWEEPS = 5
CX = 4
NY = 128
NZ = 16
KD = 8
CAP = 16
TILES = 64
ROWS = CX * 3
ASPECT = 1024.0
N_COEF = 13
F_E, F_W, A_N, A_S, C_PP, C_MP, C_PM, C_MM, LOW, INV_U, INV_V, Q_U, Q_V = range(N_COEF)
BLOCK = 32
VMEM_PREP = 60
PIVOTS = 4
PIECES = (3, 4)
V_AT, P_AT, B_AT, F_AT = 0, CX * NZ, CX * (NZ + KD), CX * (NZ + KD + 2)
T_AT, R_AT, PACK = F_AT + CX, F_AT + 8, F_AT + 16
f32 = jnp.float32
bf16 = jnp.bfloat16
VM = pl.BlockSpec(memory_space=pltpu.VMEM)
SM = pl.BlockSpec(memory_space=pltpu.SMEM)

NN = (((1,), (0,)), ((), ()))
NT = (((1,), (1,)), ((), ()))


def call(kernel, out_shape, args, scratch=(), scalars=0, flops=0, moved=0, places=None, vmem=14):
    single = not isinstance(out_shape, (list, tuple))
    shapes = [out_shape] if single else list(out_shape)
    out = pl.pallas_call(
        kernel,
        out_shape=shapes,
        in_specs=places or [SM] * scalars + [VM] * (len(args) - scalars),
        out_specs=[VM] * len(shapes),
        scratch_shapes=list(scratch),
        compiler_params=pltpu.CompilerParams(vmem_limit_bytes=int(vmem * 2**20)),
        cost_estimate=pl.CostEstimate(flops=flops, bytes_accessed=moved, transcendentals=0),
    )(*args)
    return out[0] if single else out


def sds(shape, dtype=f32):
    return jax.ShapeDtypeStruct(shape, dtype)


def dot(a, b, dims):
    return lax.dot_general(a, b, dims, preferred_element_type=f32)


def split2(x):
    high = x.astype(bf16)
    return high, (x - high.astype(f32)).astype(bf16)


def split3(x):
    high = x.astype(bf16)
    rest = x - high.astype(f32)
    middle = rest.astype(bf16)
    return high, middle, (rest - middle.astype(f32)).astype(bf16)


def dot3(a, b, dims):
    a_high, a_low = a
    b_high, b_low = b
    return dot(a_high, b_high, dims) + (dot(a_high, b_low, dims) + dot(a_low, b_high, dims))


def iota(shape, axis):
    return lax.broadcasted_iota(jnp.int32, shape, axis)


def prepare_kernel(
    at_ref, visc, probes, base, fric, tile_row, cell_row, sight,
    packed, edge_c, edge_d, asked,
    fric_in, tile_in, cell_in, sight_in, sems,
):
    rows = tile_in.shape[1]
    upper_pair = lax.rem(at_ref[0], 4) // 2
    high_row = pl.multiple_of((CX - 1) * NZ * (1 - upper_pair), NZ)
    low_row = pl.multiple_of((CX - 1) * NZ * upper_pair, NZ)
    moves = [
        (tile_row, tile_in),
        (cell_row, cell_in),
        (sight, sight_in),
        (fric, fric_in),
        (visc, packed.at[pl.ds(V_AT, CX * NZ), :]),
        (probes, packed.at[pl.ds(P_AT, CX * KD), :]),
        (base, packed.at[pl.ds(B_AT, CX * 2), :]),
        (visc.at[pl.ds(high_row, NZ), :], edge_c),
        (visc.at[pl.ds(low_row, NZ), :], edge_d),
    ]
    copies = [
        pltpu.make_async_copy(source, target, sems.at[n])
        for n, (source, target) in enumerate(moves)
    ]
    for copy in copies:
        copy.start()
    for copy in copies:
        copy.wait()
    one_hot = (iota((TILES, rows), 0) == tile_in[...]).astype(f32)
    before = (iota((rows, rows), 0) < iota((rows, rows), 1)).astype(f32).astype(bf16)
    one_hot_b = one_hot.astype(bf16)
    earlier = dot(one_hot_b, before, NN)
    rank = jnp.sum(one_hot * earlier, axis=0, keepdims=True).astype(jnp.int32)
    tail = [fric_in[...]]
    for values in (tile_in[...], rank):
        tail += [values[:, n * 128 : (n + 1) * 128].astype(f32) for n in range(rows // 128)]
    tail.append(jnp.zeros((PACK - F_AT - CX - 2 * rows // 128, NY), f32))
    packed[F_AT:PACK, :] = jnp.concatenate(tail, axis=0)
    chosen = (iota((CAP, rows), 0) == rank).astype(f32)
    values = jnp.concatenate(
        [
            chosen * cell_in[...].astype(f32),
            chosen * sight_in[0:1, :],
            chosen * sight_in[1:2, :],
            jnp.zeros((128 - 3 * CAP, rows), f32),
        ],
        axis=0,
    )
    parts = [dot(one_hot_b, part, NT) for part in split3(values)]
    asked[...] = parts[0] + (parts[1] + parts[2])


def build_coefs(visc, fric, coef, upper):
    lane = iota((NZ, NY), 1)
    layer = iota((NZ, NY), 0)

    def row(i, carry):
        centre = visc[i]
        east = visc[i + 1]
        west = visc[i - 1]

        def from_south(x):
            return pltpu.roll(x, 1, 1)

        def from_north(x):
            return pltpu.roll(x, NY - 1, 1)

        south_centre = jnp.where(lane == 0, 0.0, from_south(centre))
        north_centre = jnp.where(lane == NY - 1, 0.0, from_north(centre))
        face_e = 0.5 * (centre + east)
        face_w = 0.5 * (centre + west)
        face_n = 0.5 * (centre + north_centre)
        face_s = 0.5 * (centre + south_centre)
        coef[F_E, i - 1] = face_e
        coef[F_W, i - 1] = face_w
        coef[A_N, i - 1] = jnp.where(lane == 0, 0.0, face_s)
        coef[A_S, i - 1] = jnp.where(lane == NY - 1, 0.0, face_n)
        coef[C_PP, i - 1] = jnp.where(lane == 0, 0.0, 0.375 * (south_centre + east))
        coef[C_MP, i - 1] = jnp.where(lane == 0, 0.0, -0.375 * (south_centre + west))
        coef[C_PM, i - 1] = jnp.where(lane == NY - 1, 0.0, -0.375 * (north_centre + east))
        coef[C_MM, i - 1] = jnp.where(lane == NY - 1, 0.0, 0.375 * (north_centre + west))
        above = pltpu.roll(centre, NZ - 1, 0)
        up = jnp.where(layer == NZ - 1, 0.0, ASPECT * 0.5 * (centre + above))
        down = jnp.where(layer == 0, 0.0, pltpu.roll(up, 1, 0))
        coef[LOW, i - 1] = down
        upper[i - 1] = up
        column = (up + down) + jnp.where(layer == 0, fric[i - 1], 0.0)
        coef[INV_U, i - 1] = 4.0 * (face_e + face_w) + (face_n + face_s) + column
        coef[INV_V, i - 1] = face_e + face_w + 4.0 * (face_n + face_s) + column
        return carry

    lax.fori_loop(1, ROWS + 1, row, 0)
    inside = visc[pl.ds(1, ROWS), 0, :] > 0.0
    ratio_u = ratio_v = None
    for layer_index in range(NZ):
        pivot_u = coef[INV_U, :, layer_index, :]
        pivot_v = coef[INV_V, :, layer_index, :]
        if layer_index > 0:
            low = coef[LOW, :, layer_index, :]
            pivot_u = pivot_u - low * ratio_u
            pivot_v = pivot_v - low * ratio_v
        inverse_u = jnp.where(inside, 1.0 / pivot_u, 0.0)
        inverse_v = jnp.where(inside, 1.0 / pivot_v, 0.0)
        up = upper[:, layer_index, :]
        ratio_u = up * inverse_u
        ratio_v = up * inverse_v
        coef[INV_U, :, layer_index, :] = inverse_u
        coef[INV_V, :, layer_index, :] = inverse_v
        coef[Q_U, :, layer_index, :] = ratio_u
        coef[Q_V, :, layer_index, :] = ratio_v


def run_sweeps(coef, load, fields, load_layer, finish):
    far = NZ - 1 if load_layer == 0 else 0

    def take(which, i, layer_index):
        return jnp.broadcast_to(coef[which, i, layer_index : layer_index + 1, :], (KD, NY))

    def solve(i, right_u, right_v, last):
        forward_u, forward_v = [], []
        for k in range(NZ):
            u, v = right_u(k), right_v(k)
            if k == load_layer:
                u = load[i, 0] if u is None else u + load[i, 0]
                v = load[i, 1] if v is None else v + load[i, 1]
            if k > 0 and forward_u[-1] is not None:
                low = take(LOW, i, k)
                below_u, below_v = low * forward_u[-1], low * forward_v[-1]
                u = below_u if u is None else u + below_u
                v = below_v if v is None else v + below_v
            forward_u.append(None if u is None else u * take(INV_U, i, k))
            forward_v.append(None if v is None else v * take(INV_V, i, k))
        solved_u, solved_v = [None] * NZ, [None] * NZ
        solved_u[-1], solved_v[-1] = forward_u[-1], forward_v[-1]
        if not (last and far == NZ - 1):
            for k in range(NZ - 2, -1, -1):
                u = take(Q_U, i, k) * solved_u[k + 1]
                v = take(Q_V, i, k) * solved_v[k + 1]
                solved_u[k] = u if forward_u[k] is None else forward_u[k] + u
                solved_v[k] = v if forward_v[k] is None else forward_v[k] + v
        return solved_u, solved_v

    for sweep in range(SWEEPS):
        source, target = fields[(sweep + 1) % 2], fields[sweep % 2]
        last = sweep == SWEEPS - 1

        def row(i, carry, sweep=sweep, source=source, target=target, last=last):
            if sweep == 0:
                nothing = lambda k: None
                solved_u, solved_v = solve(i, nothing, nothing, last)
            else:

                def sides(component, k, along):
                    other = 1 - component
                    mine, east, west = (source[i + d, component, k] for d in (0, 1, -1))
                    cross_e, cross_w = (source[i + d, other, k] for d in (1, -1))
                    direct = take(F_E, i, k) * east + take(F_W, i, k) * west
                    if along:
                        direct = 4.0 * direct
                        scaled = mine
                    else:
                        scaled = 4.0 * mine
                    north = take(A_N, i, k) * scaled + (
                        take(C_PP, i, k) * cross_e + take(C_MP, i, k) * cross_w
                    )
                    south = take(A_S, i, k) * scaled + (
                        take(C_PM, i, k) * cross_e + take(C_MM, i, k) * cross_w
                    )
                    return direct + (pltpu.roll(north, NY - 1, 1) + pltpu.roll(south, 1, 1))

                solved_u, solved_v = solve(
                    i,
                    lambda k: sides(0, k, True),
                    lambda k: sides(1, k, False),
                    last,
                )
            if last:
                finish(i - CX, solved_u[far], solved_v[far])
            else:
                for k in range(NZ):
                    target[i, 0, k] = solved_u[k]
                    target[i, 1, k] = solved_v[k]
            return carry

        def pair(j, carry, row=row, sweep=sweep):
            return row(sweep + 2 * j + 1, row(sweep + 2 * j, carry))

        lax.fori_loop(0, ROWS // 2 - sweep, pair, 0)


def sides_of(at):
    odd = lax.rem(at, 2)
    return 2 - 2 * odd, 2 * odd


def state_kernel(
    at_ref, own, swap_a, swap_b, edge_c, edge_d, surface, coef, gain, visc, upper, fric, load, field_a, field_b
):
    at = at_ref[0]
    part_a, part_b = sides_of(at)
    upper_pair = lax.rem(at, 4) // 2
    visc[(ROWS + 1) * (1 - upper_pair)] = edge_c[...]
    visc[(ROWS + 1) * upper_pair] = edge_d[...]
    for part, packed in ((part_a, swap_a), (1, own), (part_b, swap_b)):
        for x in range(CX):
            i = part * CX + x
            visc[i + 1] = packed[V_AT + x * NZ : V_AT + (x + 1) * NZ, :]
            friction = packed[F_AT + x : F_AT + x + 1, :]
            fric[i] = friction
            probes = packed[P_AT + x * KD : P_AT + (x + 1) * KD, :]
            for m in range(2):
                basal = -(friction * packed[B_AT + 2 * x + m : B_AT + 2 * x + m + 1, :])
                if packed is own:
                    gain[m, x : x + 1, :] = basal
                load[i, m] = basal * probes
    build_coefs(visc, fric, coef, upper)

    def finish(x, u, v):
        surface[0, x] = u
        surface[1, x] = v

    run_sweeps(coef, load, (field_a, field_b), 0, finish)


def adjoint_kernel(
    returned, meta, coef, gain, panel_high, panel_low, hessian, moments, load, field_a, field_b
):
    beside = meta[pl.ds(3, TILES, stride=4), :]
    metas = (beside, meta[pl.ds(0, TILES, stride=4), :], pltpu.roll(beside, TILES, 1))
    for part, k in enumerate((1, 0, 2)):
        top = top_load(returned[pl.ds(k, TILES, stride=4), :], metas[part])
        for x in range(CX):
            for m in range(2):
                load[part * CX + x, m] = top[m * KD : (m + 1) * KD, x * NY : (x + 1) * NY]

    def finish(x, u, v):
        hessian[x] = gain[0, pl.ds(x, 1), :] * u + gain[1, pl.ds(x, 1), :] * v

    run_sweeps(coef, load, (field_a, field_b), NZ - 1, finish)
    whole = jnp.concatenate([hessian[x] for x in range(CX)], axis=1)
    moments[...] = dot3(split2(whole), (panel_high[...], panel_low[...]), NT)


def from_tile(value, shift):
    moved = pltpu.roll(value, -shift % TILES, 0)
    edge = TILES - 1 if shift > 0 else 0
    return jnp.where(iota(value.shape, 0) == edge, 0.0, moved)


def gram_kernel(me_ref, own, near, across, back, asked, panel_high, panel_low, payload):
    me = me_ref[0]
    count = own.shape[0] // CX
    mine = None
    for shift, block in enumerate((own, near, across, back)):
        source = me ^ shift
        flat = jnp.concatenate(
            [block[pl.ds(x, count, stride=CX), :] for x in range(CX)], axis=1
        )
        high, low = split2(flat)
        if shift == 0:
            mine = (high, low)
        at = pl.ds(pl.multiple_of(source * count, count), count)
        panel_high[at, :] = high
        panel_low[at, :] = low
    part = dot3(mine, (panel_high[...], panel_low[...]), NT)
    here = asked[...]
    payload[pl.ds(0, TILES, stride=4), :] = here
    payload[pl.ds(1, TILES, stride=4), :] = part[:, 0:128]
    payload[pl.ds(2, TILES, stride=4), :] = part[:, 128:256]
    payload[pl.ds(3, TILES, stride=4), :] = from_tile(here, -1) + pltpu.roll(
        from_tile(here, 1), TILES, 1
    )


def small_inverse(p):
    size = len(p)
    if size == 2:
        (a, b), (_, d) = p
        scale = 1.0 / (a * d - b * b)
        off = -b * scale
        return [[d * scale, off], [off, a * scale]]
    h = size // 2

    def times(x, y):
        return [
            [functools.reduce(lambda u, v: u + v, [x[i][k] * y[k][j] for k in range(h)]) for j in range(h)]
            for i in range(h)
        ]

    a = [row[:h] for row in p[:h]]
    b = [row[h:] for row in p[:h]]
    c = [row[:h] for row in p[h:]]
    d = [row[h:] for row in p[h:]]
    a_inv = small_inverse(a)
    x = times(a_inv, b)
    cx = times(c, x)
    s_inv = small_inverse([[d[i][j] - cx[i][j] for j in range(h)] for i in range(h)])
    xs = times(x, s_inv)
    x_t = [[x[j][i] for j in range(h)] for i in range(h)]
    corner = times(xs, x_t)
    top = [
        [a_inv[i][j] + corner[i][j] for j in range(h)] + [-xs[i][j] for j in range(h)]
        for i in range(h)
    ]
    bottom = [[-xs[j][i] for j in range(h)] + s_inv[i] for i in range(h)]
    return top + bottom


def invert_block(block):
    size = block.shape[0]
    row_of = iota(block.shape, 0)
    lane_of = iota(block.shape, 1)
    for k in range(0, size, PIVOTS):
        columns = [jnp.broadcast_to(block[:, k + j : k + j + 1], block.shape) for j in range(PIVOTS)]
        pivots = [[columns[j][k + i : k + i + 1, :] for j in range(PIVOTS)] for i in range(PIVOTS)]
        inverse = small_inverse(pivots)
        own_lane = (lane_of >= k) & (lane_of < k + PIVOTS)
        own = own_lane | ((row_of >= k) & (row_of < k + PIVOTS))
        rows = [
            jnp.where(
                own_lane[0:1, :],
                jnp.where(lane_of[0:1, :] == k + j, 1.0, 0.0),
                block[k + j : k + j + 1, :],
            )
            for j in range(PIVOTS)
        ]
        block = jnp.where(own, 0.0, block)
        in_rows = (row_of >= k) & (row_of < k + PIVOTS)
        for j in range(PIVOTS):
            row = functools.reduce(
                lambda u, v: u + v, [inverse[j][i] * rows[i] for i in range(PIVOTS)]
            )
            column = jnp.where(in_rows, jnp.where(row_of == k + j, -1.0, 0.0), columns[j])
            block = block - column * row
    return block


def dot_f32(a, b):
    a1, a2, a3 = split3(a)
    b1, b2, b3 = split3(b)
    small = dot(a1, b3, NN) + dot(a3, b1, NN) + dot(a2, b2, NN)
    return dot(a1, b1, NN) + ((dot(a1, b2, NN) + dot(a2, b1, NN)) + small)


def eliminate(matrix, number):
    size = matrix.shape[0]
    at = slice(number * BLOCK, (number + 1) * BLOCK)
    inverse = invert_block(matrix[at, at])
    panel = matrix[at, :]
    columns = matrix[:, at]
    lanes = iota((BLOCK, size), 1)
    own_lanes = (lanes >= number * BLOCK) & (lanes < (number + 1) * BLOCK)
    identity = (iota((BLOCK, size), 0) + number * BLOCK == lanes).astype(f32)
    rows = dot_f32(inverse, jnp.where(own_lanes, identity, panel))
    rest = matrix[...]
    all_lanes = iota((size, size), 1)
    inside = (all_lanes >= number * BLOCK) & (all_lanes < (number + 1) * BLOCK)
    matrix[...] = jnp.where(inside, 0.0, rest) - dot_f32(columns, rows)
    matrix[at, :] = rows


def first_kernel(me_ref, own, near, across, back, matrix):
    me = me_ref[0]
    for shift, block in enumerate((own, near, across, back)):
        at = pl.ds(pl.multiple_of((me ^ shift) * TILES, TILES), TILES)
        matrix[at, 0:128] = block[pl.ds(1, TILES, stride=4), :]
        matrix[at, 128:256] = block[pl.ds(2, TILES, stride=4), :]
    eliminate(matrix, 0)


def next_kernel(number, before, matrix):
    matrix[...] = before[...]
    eliminate(matrix, number)


def slot_rows(meta):
    wide = jnp.concatenate([meta, jnp.zeros((128 - TILES, 128), f32)], axis=0)
    turned = jnp.transpose(wide)
    half = CAP // 2

    def paired(at):
        return turned[at : at + half] + pltpu.roll(turned[at + half : at + CAP], TILES, 1)

    return paired(0), paired(CAP), paired(2 * CAP)


def slot_one_hot(cells):
    index = cells.astype(jnp.int32)
    at = iota((CX * NY, 128), 0)
    return jnp.concatenate(
        [(at == index[j : j + 1, :]).astype(f32).astype(bf16) for j in range(CAP // 2)], axis=1
    )


def gather_kernel(meta, surface, payload):
    cells, sight_u, sight_v = slot_rows(meta[pl.ds(0, TILES, stride=4), :])
    one_hot = slot_one_hot(cells)
    both = jnp.concatenate(
        [jnp.concatenate([surface[m, x] for x in range(CX)], axis=1) for m in range(2)], axis=0
    )
    picked = dot(jnp.concatenate(split3(both), axis=0), one_hot, NN)
    n = 2 * KD
    picked = picked[0:n] + (picked[n : 2 * n] + picked[2 * n : 3 * n])
    chunks = []
    for j in range(CAP // 2):
        at = slice(j * 128, (j + 1) * 128)
        chunks.append(
            sight_u[j : j + 1, :] * picked[0:KD, at] + sight_v[j : j + 1, :] * picked[KD:n, at]
        )
    chunks.append(jnp.zeros((128 - TILES, 128), f32))
    turned = jnp.transpose(jnp.concatenate(chunks, axis=0))
    payload[pl.ds(0, TILES, stride=4), :] = turned[0:TILES] + pltpu.roll(turned[TILES:], TILES, 1)
    for k in (1, 2):
        total = jnp.sum(meta[pl.ds(k, TILES, stride=4), :], axis=0, keepdims=True)
        payload[pl.ds(k, TILES, stride=4), :] = jnp.broadcast_to(total, (TILES, 128))
    payload[pl.ds(3, TILES, stride=4), :] = jnp.zeros((TILES, 128), f32)


def split_kernel(precision, high, low):
    high[...], low[...] = split2(precision[...])


def precision_kernel(arrived, packed, precision_high, precision_low, payload):
    rows = precision_high.shape[0]

    def line(at):
        return jnp.concatenate(
            [packed[at + n : at + n + 1, :] for n in range(rows // 128)], axis=1
        ).astype(jnp.int32)

    one_hot = (iota((128, rows), 0) == line(T_AT)).astype(f32).astype(bf16)
    rank = line(R_AT)
    mine = arrived[pl.ds(0, TILES, stride=4), :]
    turned = jnp.transpose(jnp.concatenate([mine, jnp.zeros((128 - TILES, 128), f32)], axis=0))
    spread = [dot(part, one_hot, NN) for part in split3(turned)]
    spread = spread[0] + (spread[1] + spread[2])
    predicted = jnp.zeros((KD, rows), f32)
    for s in range(CAP):
        predicted = predicted + jnp.where(rank == s, spread[s * KD : (s + 1) * KD], 0.0)
    weighted = dot3(split2(predicted), (precision_high[...], precision_low[...]), NN)
    spots = jnp.concatenate([jnp.where(rank == s, weighted, 0.0) for s in range(CAP)], axis=0)
    sent = [dot(one_hot, part, NT) for part in split3(spots)]
    sent = sent[0] + (sent[1] + sent[2])
    sent = sent[0:TILES]
    payload[pl.ds(0, TILES, stride=4), :] = sent
    payload[pl.ds(1, TILES, stride=4), :] = from_tile(sent, -1)
    payload[pl.ds(2, TILES, stride=4), :] = from_tile(sent, 1)
    payload[pl.ds(3, TILES, stride=4), :] = jnp.zeros((TILES, 128), f32)


def top_load(mine, meta):
    cells, *sights = slot_rows(meta)
    one_hot = slot_one_hot(cells)
    turned = jnp.transpose(jnp.concatenate([mine, pltpu.roll(mine, TILES, 1)], axis=0))
    loads = []
    for m in range(2):
        loads.append(
            jnp.concatenate(
                [turned[j * KD : (j + 1) * KD] * sights[m][j : j + 1, :] for j in range(CAP // 2)],
                axis=1,
            )
        )
    parts = dot(jnp.concatenate(split3(jnp.concatenate(loads, axis=0)), axis=0), one_hot, NT)
    n = 2 * KD
    return parts[0:n] + (parts[n : 2 * n] + parts[2 * n : 3 * n])


def final_kernel(parts, inverse, panel_high, panel_low, hessian, filtered, coefficients):
    solved = dot_f32(jnp.sum(parts[...], axis=0), inverse[...])
    coefficients[...] = solved
    removed = dot3(split2(solved), (panel_high[...], panel_low[...]), NN)
    for x in range(CX):
        filtered[x] = hessian[x] - removed[:, x * NY : (x + 1) * NY]


def swap(value, axis, distance, offset=0):
    count = lax.axis_size(axis)
    partner = [((i + offset) ^ distance) - offset for i in range(count)]
    return lax.ppermute(value, axis, [(i, j) for i, j in enumerate(partner) if 0 <= j < count])


def per_device(
    probes, viscosity, friction, base_velocity, obs_tile, obs_cell, sight_lines, obs_precision, basis
):
    cells = CX * NY
    me = lax.axis_index("probe").astype(jnp.int32).reshape(1)
    at = lax.axis_index("tile").astype(jnp.int32).reshape(1)
    rows = obs_cell.shape[0]
    arguments = [
        viscosity.reshape(CX * NZ, NY),
        probes.reshape(CX * KD, NY),
        base_velocity.reshape(CX * 2, NY),
        friction,
        obs_tile.reshape(1, -1),
        obs_cell.reshape(1, -1),
        sight_lines,
    ]
    own_basis = basis.reshape(-1, NY)
    others = [swap(own_basis, "probe", d) for d in (1, 2, 3)]
    packed, edge_c, edge_d, asked = call(
        prepare_kernel,
        [
            sds((PACK, NY)),
            sds((NZ, NY)),
            sds((NZ, NY)),
            sds((TILES, 128)),
        ],
        [at, *arguments],
        places=[SM] + [pl.BlockSpec(memory_space=pltpu.HBM)] * len(arguments),
        scratch=[
            pltpu.VMEM((CX, NY), f32),
            pltpu.VMEM((1, rows), jnp.int32),
            pltpu.VMEM((1, rows), jnp.int32),
            pltpu.VMEM((2, rows), f32),
            pltpu.SemaphoreType.DMA((9,)),
        ],
        flops=2 * 64 * 512 * 1000,
        moved=400000,
        vmem=VMEM_PREP,
    )
    swap_a = swap(packed, "tile", 1)
    swap_b = swap(packed, "tile", 1, 1)
    far_c = swap(edge_c, "tile", 2)
    far_d = swap(edge_d, "tile", 2, 2)
    asked, swap_a, swap_b, far_c, far_d = lax.optimization_barrier(
        (asked, swap_a, swap_b, far_c, far_d)
    )
    n_basis = 4 * basis.shape[0]
    panel_high, panel_low, request = call(
        gram_kernel,
        [sds((n_basis, cells), bf16), sds((n_basis, cells), bf16), sds((TILES * 4, 128))],
        [me, own_basis, *others, asked],
        scalars=1,
        flops=20 * 10**9,
        moved=1500000,
    )

    def exchange(value):
        return lax.all_to_all(
            value.reshape(TILES, 4, 128), "tile", split_axis=0, concat_axis=0, tiled=True
        ).reshape(TILES * 4, 128)

    meta = exchange(request)
    precision_parts = call(
        split_kernel,
        [sds(obs_precision.shape, bf16), sds(obs_precision.shape, bf16)],
        [obs_precision],
        flops=2 * 10**9,
        moved=2000000,
    )
    precision_parts, meta = lax.optimization_barrier((precision_parts, meta))

    field = pltpu.VMEM((ROWS, 2, NZ, KD, NY), f32)
    load = pltpu.VMEM((ROWS, 2, KD, NY), f32)
    surface, coef, gain = call(
        state_kernel,
        [sds((2, CX, KD, NY)), sds((N_COEF, ROWS, NZ, NY)), sds((2, CX, NY))],
        [at, packed, swap_a, swap_b, far_c, far_d],
        scalars=1,
        scratch=[
            pltpu.VMEM((ROWS + 2, NZ, NY), f32),
            pltpu.VMEM((ROWS, NZ, NY), f32),
            pltpu.VMEM((ROWS, 1, NY), f32),
            load,
            field,
            field,
        ],
        flops=40 * 16 * 44 * 1024,
        moved=2000000,
    )
    payload = call(
        gather_kernel,
        sds((TILES * 4, 128)),
        [meta, surface],
        flops=2 * 48 * 512 * 1024,
        moved=300000,
    )
    arrived = exchange(payload)
    quarters = [swap(arrived, "probe", d) for d in (1, 2, 3)]
    outgoing = call(
        precision_kernel,
        sds((TILES * 4, 128)),
        [arrived, packed, *precision_parts],
        flops=20 * 10**9,
        moved=1500000,
    )
    outgoing, *quarters = lax.optimization_barrier((outgoing, *quarters))
    returned = exchange(outgoing)
    matrix = call(
        first_kernel,
        sds((n_basis, n_basis)),
        [me, arrived, *quarters],
        scalars=1,
        flops=12 * 64 * 256 * 256,
        moved=500000,
    )
    number = 1

    def invert(matrix, pieces):
        nonlocal number
        for _ in range(pieces):
            matrix = call(
                functools.partial(next_kernel, number),
                sds((n_basis, n_basis)),
                [matrix],
                flops=12 * 64 * 256 * 256,
                moved=500000,
            )
            number += 1
        return matrix

    matrix = invert(matrix, PIECES[0])
    returned, matrix = lax.optimization_barrier((returned, matrix))
    hessian, moments = call(
        adjoint_kernel,
        [sds((CX, KD, NY)), sds((KD, n_basis))],
        [returned, meta, coef, gain, panel_high, panel_low],
        scratch=[load, field, field],
        flops=40 * 16 * 44 * 1024,
        moved=2000000,
    )
    moments, matrix = lax.optimization_barrier((moments, matrix))
    moments = moments + swap(moments, "tile", 1)
    half = TILES // 2
    parts = lax.all_to_all(
        jnp.broadcast_to(moments[None], (half, KD, n_basis)),
        "tile",
        split_axis=0,
        concat_axis=0,
        tiled=True,
        axis_index_groups=[list(range(core, TILES, 2)) for core in range(2)],
    )
    matrix = invert(matrix, PIECES[1])
    filtered, coefficients = call(
        final_kernel,
        [sds((CX, KD, NY)), sds((KD, n_basis))],
        [parts, matrix, panel_high, panel_low, hessian],
        flops=12 * 8 * 256 * 512,
        moved=800000,
    )
    return filtered, coefficients


def solution(mesh):
    in_specs = (
        P("tile", "probe", None),
        P("tile", None, None),
        P("tile", None),
        P("tile", None, None),
        P("tile", None),
        P("tile"),
        P(None, "tile"),
        P("tile", None),
        P("probe", "tile", None),
    )
    out_specs = (P("tile", "probe", None), P("probe", None))
    return jax.shard_map(
        per_device, mesh=mesh, in_specs=in_specs, out_specs=out_specs, check_vma=False
    )
```

```python
import functools

import jax
import jax.numpy as jnp
from jax import lax
from jax.experimental import pallas as pl
from jax.experimental.pallas import tpu as pltpu
from jax.sharding import PartitionSpec as P

SWEEPS = 5
CX = 4
NY = 128
NZ = 16
KD = 8
CAP = 16
HALF = 128
TILES = 64
ROWS = CX * 3
ASPECT = 1024.0
N_COEF = 13
F_E, F_W, A_N, A_S, C_PP, C_MP, C_PM, C_MM, LOW, INV_U, INV_V, Q_U, Q_V = range(N_COEF)
BLOCK = 32
VMEM_PREP = 60
PIVOTS = 4
PIECES = (3, 3)
V_AT, P_AT, B_AT, F_AT = 0, CX * NZ, CX * (NZ + KD), CX * (NZ + KD + 2)
T_AT, R_AT, PACK = F_AT + CX, F_AT + 8, F_AT + 16
f32 = jnp.float32
bf16 = jnp.bfloat16
VM = pl.BlockSpec(memory_space=pltpu.VMEM)
SM = pl.BlockSpec(memory_space=pltpu.SMEM)

NN = (((1,), (0,)), ((), ()))
NT = (((1,), (1,)), ((), ()))


def call(kernel, out_shape, args, scratch=(), scalars=0, flops=0, moved=0, places=None, vmem=14):
    single = not isinstance(out_shape, (list, tuple))
    shapes = [out_shape] if single else list(out_shape)
    out = pl.pallas_call(
        kernel,
        out_shape=shapes,
        in_specs=places or [SM] * scalars + [VM] * (len(args) - scalars),
        out_specs=[VM] * len(shapes),
        scratch_shapes=list(scratch),
        compiler_params=pltpu.CompilerParams(vmem_limit_bytes=int(vmem * 2**20)),
        cost_estimate=pl.CostEstimate(flops=flops, bytes_accessed=moved, transcendentals=0),
    )(*args)
    return out[0] if single else out


def sds(shape, dtype=f32):
    return jax.ShapeDtypeStruct(shape, dtype)


def dot(a, b, dims):
    return lax.dot_general(a, b, dims, preferred_element_type=f32)


def split2(x):
    high = x.astype(bf16)
    return high, (x - high.astype(f32)).astype(bf16)


def split3(x):
    high = x.astype(bf16)
    rest = x - high.astype(f32)
    middle = rest.astype(bf16)
    return high, middle, (rest - middle.astype(f32)).astype(bf16)


def dot3(a, b, dims):
    a_high, a_low = a
    b_high, b_low = b
    return dot(a_high, b_high, dims) + (dot(a_high, b_low, dims) + dot(a_low, b_high, dims))


def iota(shape, axis):
    return lax.broadcasted_iota(jnp.int32, shape, axis)


def prepare_kernel(
    at_ref, visc, probes, base, fric, tile_row, cell_row, sight,
    packed, edge_c, edge_d, asked,
    fric_in, tile_in, cell_in, sight_in, sems,
):
    rows = tile_in.shape[1]
    upper_pair = lax.rem(at_ref[0], 4) // 2
    high_row = pl.multiple_of((CX - 1) * NZ * (1 - upper_pair), NZ)
    low_row = pl.multiple_of((CX - 1) * NZ * upper_pair, NZ)
    moves = [
        (tile_row, tile_in),
        (cell_row, cell_in),
        (sight, sight_in),
        (fric, fric_in),
        (visc, packed.at[pl.ds(V_AT, CX * NZ), :]),
        (probes, packed.at[pl.ds(P_AT, CX * KD), :]),
        (base, packed.at[pl.ds(B_AT, CX * 2), :]),
        (visc.at[pl.ds(high_row, NZ), :], edge_c),
        (visc.at[pl.ds(low_row, NZ), :], edge_d),
    ]
    copies = [
        pltpu.make_async_copy(source, target, sems.at[n])
        for n, (source, target) in enumerate(moves)
    ]
    for copy in copies:
        copy.start()
    for copy in copies:
        copy.wait()
    one_hot = (iota((TILES, rows), 0) == tile_in[...]).astype(f32)
    before = (iota((rows, rows), 0) < iota((rows, rows), 1)).astype(f32).astype(bf16)
    one_hot_b = one_hot.astype(bf16)
    earlier = dot(one_hot_b, before, NN)
    rank = jnp.sum(one_hot * earlier, axis=0, keepdims=True).astype(jnp.int32)
    tail = [fric_in[...]]
    for values in (tile_in[...], rank):
        tail += [values[:, n * 128 : (n + 1) * 128].astype(f32) for n in range(rows // 128)]
    tail.append(jnp.zeros((PACK - F_AT - CX - 2 * rows // 128, NY), f32))
    packed[F_AT:PACK, :] = jnp.concatenate(tail, axis=0)
    chosen = (iota((CAP, rows), 0) == rank).astype(f32)
    values = jnp.concatenate(
        [
            chosen * cell_in[...].astype(f32),
            chosen * sight_in[0:1, :],
            chosen * sight_in[1:2, :],
            jnp.zeros((128 - 3 * CAP, rows), f32),
        ],
        axis=0,
    )
    parts = [dot(one_hot_b, part, NT) for part in split3(values)]
    asked[...] = parts[0] + (parts[1] + parts[2])


def build_coefs(visc, fric, coef, upper):
    lane = iota((NZ, NY), 1)
    layer = iota((NZ, NY), 0)

    def row(i, carry):
        centre = visc[i]
        east = visc[i + 1]
        west = visc[i - 1]

        def from_south(x):
            return pltpu.roll(x, 1, 1)

        def from_north(x):
            return pltpu.roll(x, NY - 1, 1)

        south_centre = jnp.where(lane == 0, 0.0, from_south(centre))
        north_centre = jnp.where(lane == NY - 1, 0.0, from_north(centre))
        face_e = 0.5 * (centre + east)
        face_w = 0.5 * (centre + west)
        face_n = 0.5 * (centre + north_centre)
        face_s = 0.5 * (centre + south_centre)
        coef[F_E, i - 1] = face_e
        coef[F_W, i - 1] = face_w
        coef[A_N, i - 1] = jnp.where(lane == 0, 0.0, face_s)
        coef[A_S, i - 1] = jnp.where(lane == NY - 1, 0.0, face_n)
        coef[C_PP, i - 1] = jnp.where(lane == 0, 0.0, 0.375 * (south_centre + east))
        coef[C_MP, i - 1] = jnp.where(lane == 0, 0.0, -0.375 * (south_centre + west))
        coef[C_PM, i - 1] = jnp.where(lane == NY - 1, 0.0, -0.375 * (north_centre + east))
        coef[C_MM, i - 1] = jnp.where(lane == NY - 1, 0.0, 0.375 * (north_centre + west))
        above = pltpu.roll(centre, NZ - 1, 0)
        up = jnp.where(layer == NZ - 1, 0.0, ASPECT * 0.5 * (centre + above))
        down = jnp.where(layer == 0, 0.0, pltpu.roll(up, 1, 0))
        coef[LOW, i - 1] = down
        upper[i - 1] = up
        column = (up + down) + jnp.where(layer == 0, fric[i - 1], 0.0)
        coef[INV_U, i - 1] = 4.0 * (face_e + face_w) + (face_n + face_s) + column
        coef[INV_V, i - 1] = face_e + face_w + 4.0 * (face_n + face_s) + column
        return carry

    lax.fori_loop(1, ROWS + 1, row, 0)
    inside = visc[pl.ds(1, ROWS), 0, :] > 0.0
    ratio_u = ratio_v = None
    for layer_index in range(NZ):
        pivot_u = coef[INV_U, :, layer_index, :]
        pivot_v = coef[INV_V, :, layer_index, :]
        if layer_index > 0:
            low = coef[LOW, :, layer_index, :]
            pivot_u = pivot_u - low * ratio_u
            pivot_v = pivot_v - low * ratio_v
        inverse_u = jnp.where(inside, 1.0 / pivot_u, 0.0)
        inverse_v = jnp.where(inside, 1.0 / pivot_v, 0.0)
        up = upper[:, layer_index, :]
        ratio_u = up * inverse_u
        ratio_v = up * inverse_v
        coef[INV_U, :, layer_index, :] = inverse_u
        coef[INV_V, :, layer_index, :] = inverse_v
        coef[Q_U, :, layer_index, :] = ratio_u
        coef[Q_V, :, layer_index, :] = ratio_v


def run_sweeps(coef, load, fields, load_layer, finish):
    far = NZ - 1 if load_layer == 0 else 0

    def take(which, i, layer_index):
        return jnp.broadcast_to(coef[which, i, layer_index : layer_index + 1, :], (KD, NY))

    def solve(i, right_u, right_v, last):
        forward_u, forward_v = [], []
        for k in range(NZ):
            u, v = right_u(k), right_v(k)
            if k == load_layer:
                u = load[i, 0] if u is None else u + load[i, 0]
                v = load[i, 1] if v is None else v + load[i, 1]
            if k > 0 and forward_u[-1] is not None:
                low = take(LOW, i, k)
                below_u, below_v = low * forward_u[-1], low * forward_v[-1]
                u = below_u if u is None else u + below_u
                v = below_v if v is None else v + below_v
            forward_u.append(None if u is None else u * take(INV_U, i, k))
            forward_v.append(None if v is None else v * take(INV_V, i, k))
        solved_u, solved_v = [None] * NZ, [None] * NZ
        solved_u[-1], solved_v[-1] = forward_u[-1], forward_v[-1]
        if not (last and far == NZ - 1):
            for k in range(NZ - 2, -1, -1):
                u = take(Q_U, i, k) * solved_u[k + 1]
                v = take(Q_V, i, k) * solved_v[k + 1]
                solved_u[k] = u if forward_u[k] is None else forward_u[k] + u
                solved_v[k] = v if forward_v[k] is None else forward_v[k] + v
        return solved_u, solved_v

    for sweep in range(SWEEPS):
        source, target = fields[(sweep + 1) % 2], fields[sweep % 2]
        last = sweep == SWEEPS - 1

        def row(i, carry, sweep=sweep, source=source, target=target, last=last):
            if sweep == 0:
                nothing = lambda k: None
                solved_u, solved_v = solve(i, nothing, nothing, last)
            else:

                def sides(component, k, along):
                    other = 1 - component
                    mine, east, west = (source[i + d, component, k] for d in (0, 1, -1))
                    cross_e, cross_w = (source[i + d, other, k] for d in (1, -1))
                    direct = take(F_E, i, k) * east + take(F_W, i, k) * west
                    if along:
                        direct = 4.0 * direct
                        scaled = mine
                    else:
                        scaled = 4.0 * mine
                    north = take(A_N, i, k) * scaled + (
                        take(C_PP, i, k) * cross_e + take(C_MP, i, k) * cross_w
                    )
                    south = take(A_S, i, k) * scaled + (
                        take(C_PM, i, k) * cross_e + take(C_MM, i, k) * cross_w
                    )
                    return direct + (pltpu.roll(north, NY - 1, 1) + pltpu.roll(south, 1, 1))

                solved_u, solved_v = solve(
                    i,
                    lambda k: sides(0, k, True),
                    lambda k: sides(1, k, False),
                    last,
                )
            if last:
                finish(i - CX, solved_u[far], solved_v[far])
            else:
                for k in range(NZ):
                    target[i, 0, k] = solved_u[k]
                    target[i, 1, k] = solved_v[k]
            return carry

        def pair(j, carry, row=row, sweep=sweep):
            return row(sweep + 2 * j + 1, row(sweep + 2 * j, carry))

        lax.fori_loop(0, ROWS // 2 - sweep, pair, 0)


def sides_of(at):
    odd = lax.rem(at, 2)
    return 2 - 2 * odd, 2 * odd


def state_kernel(
    at_ref, own, swap_a, swap_b, edge_c, edge_d, surface, coef, gain, visc, upper, fric, load, field_a, field_b
):
    at = at_ref[0]
    part_a, part_b = sides_of(at)
    upper_pair = lax.rem(at, 4) // 2
    visc[(ROWS + 1) * (1 - upper_pair)] = edge_c[...]
    visc[(ROWS + 1) * upper_pair] = edge_d[...]
    for part, packed in ((part_a, swap_a), (1, own), (part_b, swap_b)):
        for x in range(CX):
            i = part * CX + x
            visc[i + 1] = packed[V_AT + x * NZ : V_AT + (x + 1) * NZ, :]
            friction = packed[F_AT + x : F_AT + x + 1, :]
            fric[i] = friction
            probes = packed[P_AT + x * KD : P_AT + (x + 1) * KD, :]
            for m in range(2):
                basal = -(friction * packed[B_AT + 2 * x + m : B_AT + 2 * x + m + 1, :])
                if packed is own:
                    gain[m, x : x + 1, :] = basal
                load[i, m] = basal * probes
    build_coefs(visc, fric, coef, upper)

    def finish(x, u, v):
        surface[0, x] = u
        surface[1, x] = v

    run_sweeps(coef, load, (field_a, field_b), 0, finish)


def adjoint_kernel(
    returned, meta, coef, gain, panel_high, panel_low, hessian, moments, load, field_a, field_b
):
    beside = meta[:, 1, :]
    metas = (beside, meta[:, 0, :], pltpu.roll(beside, TILES, 1))
    for part, k in enumerate((1, 0, 2)):
        top = top_load(returned[pl.ds(k, TILES, stride=4), :], metas[part])
        for x in range(CX):
            for m in range(2):
                load[part * CX + x, m] = top[m * KD : (m + 1) * KD, x * NY : (x + 1) * NY]

    def finish(x, u, v):
        hessian[x] = gain[0, pl.ds(x, 1), :] * u + gain[1, pl.ds(x, 1), :] * v

    run_sweeps(coef, load, (field_a, field_b), NZ - 1, finish)
    whole = jnp.concatenate([hessian[x] for x in range(CX)], axis=1)
    moments[...] = dot3(split2(whole), (panel_high[...], panel_low[...]), NT)


def from_tile(value, shift):
    moved = pltpu.roll(value, -shift % TILES, 0)
    edge = TILES - 1 if shift > 0 else 0
    return jnp.where(iota(value.shape, 0) == edge, 0.0, moved)


def gram_kernel(
    me_ref, own, near, across, back, asked, panel_high, panel_low, payload, gram_11, gram_12, gram_22
):
    me = me_ref[0]
    count = own.shape[0] // CX
    for shift, block in enumerate((own, near, across, back)):
        source = me ^ shift
        flat = jnp.concatenate(
            [block[pl.ds(x, count, stride=CX), :] for x in range(CX)], axis=1
        )
        at = pl.ds(pl.multiple_of(source * count, count), count)
        panel_high[at, :], panel_low[at, :] = split2(flat)
    upper = panel_high[0:HALF, :], panel_low[0:HALF, :]
    lower = panel_high[HALF:, :], panel_low[HALF:, :]
    gram_11[...] = dot3(upper, upper, NT)
    gram_12[...] = dot3(upper, lower, NT)
    gram_22[...] = dot3(lower, lower, NT)
    here = asked[...]
    payload[:, 0, :] = here
    payload[:, 1, :] = from_tile(here, -1) + pltpu.roll(from_tile(here, 1), TILES, 1)
    for k, n, block in gram_lines(gram_11, gram_12, gram_22):
        payload[:, k, :] = block[pl.ds(n, TILES, stride=2), :]


def gram_lines(gram_11, gram_12, gram_22):
    return (2, 0, gram_11), (3, 0, gram_12), (4, 1, gram_11), (5, 1, gram_12), (6, 0, gram_22), (7, 1, gram_22)


def small_inverse(p):
    size = len(p)
    if size == 2:
        (a, b), (_, d) = p
        scale = 1.0 / (a * d - b * b)
        off = -b * scale
        return [[d * scale, off], [off, a * scale]]
    h = size // 2

    def times(x, y):
        return [
            [functools.reduce(lambda u, v: u + v, [x[i][k] * y[k][j] for k in range(h)]) for j in range(h)]
            for i in range(h)
        ]

    a = [row[:h] for row in p[:h]]
    b = [row[h:] for row in p[:h]]
    c = [row[:h] for row in p[h:]]
    d = [row[h:] for row in p[h:]]
    a_inv = small_inverse(a)
    x = times(a_inv, b)
    cx = times(c, x)
    s_inv = small_inverse([[d[i][j] - cx[i][j] for j in range(h)] for i in range(h)])
    xs = times(x, s_inv)
    x_t = [[x[j][i] for j in range(h)] for i in range(h)]
    corner = times(xs, x_t)
    top = [
        [a_inv[i][j] + corner[i][j] for j in range(h)] + [-xs[i][j] for j in range(h)]
        for i in range(h)
    ]
    bottom = [[-xs[j][i] for j in range(h)] + s_inv[i] for i in range(h)]
    return top + bottom


def invert_block(block):
    size = block.shape[0]
    row_of = iota(block.shape, 0)
    lane_of = iota(block.shape, 1)
    for k in range(0, size, PIVOTS):
        columns = [jnp.broadcast_to(block[:, k + j : k + j + 1], block.shape) for j in range(PIVOTS)]
        pivots = [[columns[j][k + i : k + i + 1, :] for j in range(PIVOTS)] for i in range(PIVOTS)]
        inverse = small_inverse(pivots)
        own_lane = (lane_of >= k) & (lane_of < k + PIVOTS)
        own = own_lane | ((row_of >= k) & (row_of < k + PIVOTS))
        rows = [
            jnp.where(
                own_lane[0:1, :],
                jnp.where(lane_of[0:1, :] == k + j, 1.0, 0.0),
                block[k + j : k + j + 1, :],
            )
            for j in range(PIVOTS)
        ]
        block = jnp.where(own, 0.0, block)
        in_rows = (row_of >= k) & (row_of < k + PIVOTS)
        for j in range(PIVOTS):
            row = functools.reduce(
                lambda u, v: u + v, [inverse[j][i] * rows[i] for i in range(PIVOTS)]
            )
            column = jnp.where(in_rows, jnp.where(row_of == k + j, -1.0, 0.0), columns[j])
            block = block - column * row
    return block


def dot_f32(a, b):
    a1, a2, a3 = split3(a)
    b1, b2, b3 = split3(b)
    small = dot(a1, b3, NN) + dot(a3, b1, NN) + dot(a2, b2, NN)
    return dot(a1, b1, NN) + ((dot(a1, b2, NN) + dot(a2, b1, NN)) + small)


def eliminate(matrix, number):
    size = matrix.shape[0]
    at = slice(number * BLOCK, (number + 1) * BLOCK)
    inverse = invert_block(matrix[at, at])
    panel = matrix[at, :]
    columns = matrix[:, at]
    lanes = iota((BLOCK, size), 1)
    own_lanes = (lanes >= number * BLOCK) & (lanes < (number + 1) * BLOCK)
    identity = (iota((BLOCK, size), 0) + number * BLOCK == lanes).astype(f32)
    rows = dot_f32(inverse, jnp.where(own_lanes, identity, panel))
    rest = matrix[...]
    all_lanes = iota((size, size), 1)
    inside = (all_lanes >= number * BLOCK) & (all_lanes < (number + 1) * BLOCK)
    matrix[...] = jnp.where(inside, 0.0, rest) - dot_f32(columns, rows)
    matrix[at, :] = rows


def first_kernel(arrived, matrix, gram_11, gram_12, gram_22):
    for k, n, block in gram_lines(gram_11, gram_12, gram_22):
        block[pl.ds(n, TILES, stride=2), :] = arrived[:, k, :]
    matrix[0:HALF, 0:HALF] = gram_11[...]
    matrix[0:HALF, HALF:] = gram_12[...]
    matrix[HALF:, 0:HALF] = jnp.transpose(gram_12[...])
    matrix[HALF:, HALF:] = gram_22[...]
    eliminate(matrix, 0)


def next_kernel(number, before, matrix):
    matrix[...] = before[...]
    eliminate(matrix, number)


def slot_rows(meta):
    wide = jnp.concatenate([meta, jnp.zeros((128 - TILES, 128), f32)], axis=0)
    turned = jnp.transpose(wide)
    half = CAP // 2

    def paired(at):
        return turned[at : at + half] + pltpu.roll(turned[at + half : at + CAP], TILES, 1)

    return paired(0), paired(CAP), paired(2 * CAP)


def slot_one_hot(cells):
    index = cells.astype(jnp.int32)
    at = iota((CX * NY, 128), 0)
    return jnp.concatenate(
        [(at == index[j : j + 1, :]).astype(f32).astype(bf16) for j in range(CAP // 2)], axis=1
    )


def gather_kernel(meta, surface, payload):
    cells, sight_u, sight_v = slot_rows(meta[:, 0, :])
    one_hot = slot_one_hot(cells)
    both = jnp.concatenate(
        [jnp.concatenate([surface[m, x] for x in range(CX)], axis=1) for m in range(2)], axis=0
    )
    picked = dot(jnp.concatenate(split3(both), axis=0), one_hot, NN)
    n = 2 * KD
    picked = picked[0:n] + (picked[n : 2 * n] + picked[2 * n : 3 * n])
    chunks = []
    for j in range(CAP // 2):
        at = slice(j * 128, (j + 1) * 128)
        chunks.append(
            sight_u[j : j + 1, :] * picked[0:KD, at] + sight_v[j : j + 1, :] * picked[KD:n, at]
        )
    chunks.append(jnp.zeros((128 - TILES, 128), f32))
    turned = jnp.transpose(jnp.concatenate(chunks, axis=0))
    payload[...] = jnp.broadcast_to(jnp.sum(meta[...], axis=0, keepdims=True), payload.shape)
    payload[:, 0, :] = turned[0:TILES] + pltpu.roll(turned[TILES:], TILES, 1)


def split_kernel(precision, high, low):
    high[...], low[...] = split2(precision[...])


def precision_kernel(arrived, packed, precision_high, precision_low, payload):
    rows = precision_high.shape[0]

    def line(at):
        return jnp.concatenate(
            [packed[at + n : at + n + 1, :] for n in range(rows // 128)], axis=1
        ).astype(jnp.int32)

    one_hot = (iota((128, rows), 0) == line(T_AT)).astype(f32).astype(bf16)
    rank = line(R_AT)
    mine = arrived[:, 0, :]
    turned = jnp.transpose(jnp.concatenate([mine, jnp.zeros((128 - TILES, 128), f32)], axis=0))
    spread = [dot(part, one_hot, NN) for part in split3(turned)]
    spread = spread[0] + (spread[1] + spread[2])
    predicted = jnp.zeros((KD, rows), f32)
    for s in range(CAP):
        predicted = predicted + jnp.where(rank == s, spread[s * KD : (s + 1) * KD], 0.0)
    weighted = dot3(split2(predicted), (precision_high[...], precision_low[...]), NN)
    spots = jnp.concatenate([jnp.where(rank == s, weighted, 0.0) for s in range(CAP)], axis=0)
    sent = [dot(one_hot, part, NT) for part in split3(spots)]
    sent = sent[0] + (sent[1] + sent[2])
    sent = sent[0:TILES]
    payload[pl.ds(0, TILES, stride=4), :] = sent
    payload[pl.ds(1, TILES, stride=4), :] = from_tile(sent, -1)
    payload[pl.ds(2, TILES, stride=4), :] = from_tile(sent, 1)
    payload[pl.ds(3, TILES, stride=4), :] = jnp.zeros((TILES, 128), f32)


def top_load(mine, meta):
    cells, *sights = slot_rows(meta)
    one_hot = slot_one_hot(cells)
    turned = jnp.transpose(jnp.concatenate([mine, pltpu.roll(mine, TILES, 1)], axis=0))
    loads = []
    for m in range(2):
        loads.append(
            jnp.concatenate(
                [turned[j * KD : (j + 1) * KD] * sights[m][j : j + 1, :] for j in range(CAP // 2)],
                axis=1,
            )
        )
    parts = dot(jnp.concatenate(split3(jnp.concatenate(loads, axis=0)), axis=0), one_hot, NT)
    n = 2 * KD
    return parts[0:n] + (parts[n : 2 * n] + parts[2 * n : 3 * n])


def copies_kernel(own, other, copies):
    copies[...] = jnp.broadcast_to((own[...] + other[...])[None], copies.shape)


def last_kernel(number, before, panel_high, panel_low, high, middle, low, spread_high, spread_low, matrix):
    matrix[...] = before[...]
    eliminate(matrix, number)
    inverse = matrix[...]
    high[...], middle[...], low[...] = split3(inverse)
    spread = dot3(split2(inverse), (panel_high[...], panel_low[...]), NN)
    spread_high[...], spread_low[...] = split2(spread)


def final_kernel(parts, high, middle, low, spread_high, spread_low, hessian, filtered, coefficients):
    a1, a2, a3 = split3(jnp.sum(parts[...], axis=0))
    removed = dot3((a1, a2), (spread_high[...], spread_low[...]), NN)
    b1, b2, b3 = high[...], middle[...], low[...]
    small = dot(a1, b3, NN) + dot(a3, b1, NN) + dot(a2, b2, NN)
    coefficients[...] = dot(a1, b1, NN) + ((dot(a1, b2, NN) + dot(a2, b1, NN)) + small)
    for x in range(CX):
        filtered[x] = hessian[x] - removed[:, x * NY : (x + 1) * NY]


def swap(value, axis, distance, offset=0):
    count = lax.axis_size(axis)
    partner = [((i + offset) ^ distance) - offset for i in range(count)]
    return lax.ppermute(value, axis, [(i, j) for i, j in enumerate(partner) if 0 <= j < count])


def per_device(
    probes, viscosity, friction, base_velocity, obs_tile, obs_cell, sight_lines, obs_precision, basis
):
    cells = CX * NY
    me = lax.axis_index("probe").astype(jnp.int32).reshape(1)
    at = lax.axis_index("tile").astype(jnp.int32).reshape(1)
    rows = obs_cell.shape[0]
    arguments = [
        viscosity.reshape(CX * NZ, NY),
        probes.reshape(CX * KD, NY),
        base_velocity.reshape(CX * 2, NY),
        friction,
        obs_tile.reshape(1, -1),
        obs_cell.reshape(1, -1),
        sight_lines,
    ]
    own_basis = basis.reshape(-1, NY)
    others = [swap(own_basis, "probe", d) for d in (1, 2, 3)]
    packed, edge_c, edge_d, asked = call(
        prepare_kernel,
        [
            sds((PACK, NY)),
            sds((NZ, NY)),
            sds((NZ, NY)),
            sds((TILES, 128)),
        ],
        [at, *arguments],
        places=[SM] + [pl.BlockSpec(memory_space=pltpu.HBM)] * len(arguments),
        scratch=[
            pltpu.VMEM((CX, NY), f32),
            pltpu.VMEM((1, rows), jnp.int32),
            pltpu.VMEM((1, rows), jnp.int32),
            pltpu.VMEM((2, rows), f32),
            pltpu.SemaphoreType.DMA((9,)),
        ],
        flops=2 * 64 * 512 * 1000,
        moved=400000,
        vmem=VMEM_PREP,
    )
    swap_a = swap(packed, "tile", 1)
    swap_b = swap(packed, "tile", 1, 1)
    far_c = swap(edge_c, "tile", 2)
    far_d = swap(edge_d, "tile", 2, 2)
    asked, swap_b, far_d = lax.optimization_barrier((asked, swap_b, far_d))
    n_basis = 4 * basis.shape[0]
    panel_high, panel_low, request = call(
        gram_kernel,
        [sds((n_basis, cells), bf16), sds((n_basis, cells), bf16), sds((TILES, 8, 128))],
        [me, own_basis, *others, asked],
        scratch=[pltpu.VMEM((HALF, HALF), f32)] * 3,
        scalars=1,
        flops=20 * 10**9,
        moved=1500000,
    )

    def exchange(value):
        return lax.all_to_all(value, "tile", split_axis=0, concat_axis=0, tiled=True)

    meta = exchange(request)
    precision_parts = call(
        split_kernel,
        [sds(obs_precision.shape, bf16), sds(obs_precision.shape, bf16)],
        [obs_precision],
        flops=2 * 10**9,
        moved=2000000,
    )
    precision_parts, meta = lax.optimization_barrier((precision_parts, meta))

    field = pltpu.VMEM((ROWS, 2, NZ, KD, NY), f32)
    load = pltpu.VMEM((ROWS, 2, KD, NY), f32)
    surface, coef, gain = call(
        state_kernel,
        [sds((2, CX, KD, NY)), sds((N_COEF, ROWS, NZ, NY)), sds((2, CX, NY))],
        [at, packed, swap_a, swap_b, far_c, far_d],
        scalars=1,
        scratch=[
            pltpu.VMEM((ROWS + 2, NZ, NY), f32),
            pltpu.VMEM((ROWS, NZ, NY), f32),
            pltpu.VMEM((ROWS, 1, NY), f32),
            load,
            field,
            field,
        ],
        flops=40 * 16 * 44 * 1024,
        moved=2000000,
    )
    payload = call(
        gather_kernel,
        sds((TILES, 8, 128)),
        [meta, surface],
        flops=2 * 48 * 512 * 1024,
        moved=300000,
    )
    arrived = exchange(payload)
    outgoing = call(
        precision_kernel,
        sds((TILES * 4, 128)),
        [arrived, packed, *precision_parts],
        flops=20 * 10**9,
        moved=1500000,
    )
    returned = exchange(outgoing.reshape(TILES, 4, 128)).reshape(TILES * 4, 128)
    matrix = call(
        first_kernel,
        sds((n_basis, n_basis)),
        [arrived],
        scratch=[pltpu.VMEM((HALF, HALF), f32)] * 3,
        flops=12 * 64 * 256 * 256,
        moved=500000,
    )
    number = 1

    def invert(matrix, pieces):
        nonlocal number
        for _ in range(pieces):
            matrix = call(
                functools.partial(next_kernel, number),
                sds((n_basis, n_basis)),
                [matrix],
                flops=12 * 64 * 256 * 256,
                moved=500000,
            )
            number += 1
        return matrix

    matrix = invert(matrix, PIECES[0])
    returned, matrix = lax.optimization_barrier((returned, matrix))
    hessian, moments = call(
        adjoint_kernel,
        [sds((CX, KD, NY)), sds((KD, n_basis))],
        [returned, meta, coef, gain, panel_high, panel_low],
        scratch=[load, field, field],
        flops=40 * 16 * 44 * 1024,
        moved=2000000,
    )
    moments, matrix = lax.optimization_barrier((moments, matrix))
    half = TILES // 2
    copies = call(
        copies_kernel,
        sds((half, KD, n_basis)),
        [moments, swap(moments, "tile", 1)],
        flops=half * KD * n_basis,
        moved=4 * half * KD * n_basis,
    )
    parts = lax.all_to_all(
        copies,
        "tile",
        split_axis=0,
        concat_axis=0,
        tiled=True,
        axis_index_groups=[list(range(core, TILES, 2)) for core in range(2)],
    )
    matrix = invert(matrix, PIECES[1])
    inverse = call(
        functools.partial(last_kernel, number),
        [sds((n_basis, n_basis), bf16)] * 3 + [sds((n_basis, cells), bf16)] * 2,
        [matrix, panel_high, panel_low],
        scratch=[pltpu.VMEM((n_basis, n_basis), f32)],
        flops=12 * 64 * 256 * 256 + 6 * 256 * 256 * 512,
        moved=1500000,
    )
    filtered, coefficients = call(
        final_kernel,
        [sds((CX, KD, NY)), sds((KD, n_basis))],
        [parts, *inverse, hessian],
        flops=12 * 8 * 256 * 512,
        moved=800000,
    )
    return filtered, coefficients


def solution(mesh):
    in_specs = (
        P("tile", "probe", None),
        P("tile", None, None),
        P("tile", None),
        P("tile", None, None),
        P("tile", None),
        P("tile"),
        P(None, "tile"),
        P("tile", None),
        P("probe", "tile", None),
    )
    out_specs = (P("tile", "probe", None), P("probe", None))
    return jax.shard_map(
        per_device, mesh=mesh, in_specs=in_specs, out_specs=out_specs, check_vma=False
    )
```

```python
import functools

import jax
import jax.numpy as jnp
from jax import lax
from jax.experimental import pallas as pl
from jax.experimental.pallas import tpu as pltpu
from jax.sharding import PartitionSpec as P

SWEEPS = 5
CX = 4
NY = 128
NZ = 16
KD = 8
CAP = 16
HALF = 128
TILES = 64
ROWS = CX * 3
ASPECT = 1024.0
N_COEF = 13
F_E, F_W, A_N, A_S, C_PP, C_MP, C_PM, C_MM, LOW, INV_U, INV_V, Q_U, Q_V = range(N_COEF)
BLOCK = 32
VMEM_PREP = 60
PIVOTS = 4
PIECES = (3, 3)
V_AT, P_AT, B_AT, F_AT = 0, CX * NZ, CX * (NZ + KD), CX * (NZ + KD + 2)
PACK = F_AT + 8
f32 = jnp.float32
bf16 = jnp.bfloat16
VM = pl.BlockSpec(memory_space=pltpu.VMEM)
SM = pl.BlockSpec(memory_space=pltpu.SMEM)

NN = (((1,), (0,)), ((), ()))
NT = (((1,), (1,)), ((), ()))


def call(kernel, out_shape, args, scratch=(), scalars=0, flops=0, moved=0, places=None, vmem=14):
    single = not isinstance(out_shape, (list, tuple))
    shapes = [out_shape] if single else list(out_shape)
    out = pl.pallas_call(
        kernel,
        out_shape=shapes,
        in_specs=places or [SM] * scalars + [VM] * (len(args) - scalars),
        out_specs=[VM] * len(shapes),
        scratch_shapes=list(scratch),
        compiler_params=pltpu.CompilerParams(vmem_limit_bytes=int(vmem * 2**20)),
        cost_estimate=pl.CostEstimate(flops=flops, bytes_accessed=moved, transcendentals=0),
    )(*args)
    return out[0] if single else out


def sds(shape, dtype=f32):
    return jax.ShapeDtypeStruct(shape, dtype)


def dot(a, b, dims):
    return lax.dot_general(a, b, dims, preferred_element_type=f32)


def split2(x):
    high = x.astype(bf16)
    return high, (x - high.astype(f32)).astype(bf16)


def split3(x):
    high = x.astype(bf16)
    rest = x - high.astype(f32)
    middle = rest.astype(bf16)
    return high, middle, (rest - middle.astype(f32)).astype(bf16)


def dot3(a, b, dims):
    a_high, a_low = a
    b_high, b_low = b
    return dot(a_high, b_high, dims) + (dot(a_high, b_low, dims) + dot(a_low, b_high, dims))


def iota(shape, axis):
    return lax.broadcasted_iota(jnp.int32, shape, axis)


def prepare_kernel(
    at_ref, visc, probes, base, fric, packed, edge_c, edge_d, fric_in, sems
):
    upper_pair = lax.rem(at_ref[0], 4) // 2
    high_row = pl.multiple_of((CX - 1) * NZ * (1 - upper_pair), NZ)
    low_row = pl.multiple_of((CX - 1) * NZ * upper_pair, NZ)
    moves = [
        (fric, fric_in),
        (visc, packed.at[pl.ds(V_AT, CX * NZ), :]),
        (probes, packed.at[pl.ds(P_AT, CX * KD), :]),
        (base, packed.at[pl.ds(B_AT, CX * 2), :]),
        (visc.at[pl.ds(high_row, NZ), :], edge_c),
        (visc.at[pl.ds(low_row, NZ), :], edge_d),
    ]
    copies = [
        pltpu.make_async_copy(source, target, sems.at[n])
        for n, (source, target) in enumerate(moves)
    ]
    for copy in copies:
        copy.start()
    for copy in copies:
        copy.wait()
    packed[F_AT:PACK, :] = jnp.concatenate(
        [fric_in[...], jnp.zeros((PACK - F_AT - CX, NY), f32)], axis=0
    )


def meta_kernel(tile_in, cell_in, sight_in, basis, asked, slots, own_basis):
    own_basis[...] = basis[...]
    rows = tile_in.shape[1]
    one_hot = (iota((TILES, rows), 0) == tile_in[...]).astype(f32)
    before = (iota((rows, rows), 0) < iota((rows, rows), 1)).astype(f32).astype(bf16)
    one_hot_b = one_hot.astype(bf16)
    earlier = dot(one_hot_b, before, NN)
    rank = jnp.sum(one_hot * earlier, axis=0, keepdims=True).astype(jnp.int32)
    slots[0:1, :] = tile_in[...]
    slots[1:2, :] = rank
    chosen = (iota((CAP, rows), 0) == rank).astype(f32)
    values = jnp.concatenate(
        [
            chosen * cell_in[...].astype(f32),
            chosen * sight_in[0:1, :],
            chosen * sight_in[1:2, :],
            jnp.zeros((128 - 3 * CAP, rows), f32),
        ],
        axis=0,
    )
    parts = [dot(one_hot_b, part, NT) for part in split3(values)]
    asked[...] = parts[0] + (parts[1] + parts[2])


def build_coefs(visc, fric, coef, upper):
    lane = iota((NZ, NY), 1)
    layer = iota((NZ, NY), 0)

    def row(i, carry):
        centre = visc[i]
        east = visc[i + 1]
        west = visc[i - 1]

        def from_south(x):
            return pltpu.roll(x, 1, 1)

        def from_north(x):
            return pltpu.roll(x, NY - 1, 1)

        south_centre = jnp.where(lane == 0, 0.0, from_south(centre))
        north_centre = jnp.where(lane == NY - 1, 0.0, from_north(centre))
        face_e = 0.5 * (centre + east)
        face_w = 0.5 * (centre + west)
        face_n = 0.5 * (centre + north_centre)
        face_s = 0.5 * (centre + south_centre)
        coef[F_E, i - 1] = face_e
        coef[F_W, i - 1] = face_w
        coef[A_N, i - 1] = jnp.where(lane == 0, 0.0, face_s)
        coef[A_S, i - 1] = jnp.where(lane == NY - 1, 0.0, face_n)
        coef[C_PP, i - 1] = jnp.where(lane == 0, 0.0, 0.375 * (south_centre + east))
        coef[C_MP, i - 1] = jnp.where(lane == 0, 0.0, -0.375 * (south_centre + west))
        coef[C_PM, i - 1] = jnp.where(lane == NY - 1, 0.0, -0.375 * (north_centre + east))
        coef[C_MM, i - 1] = jnp.where(lane == NY - 1, 0.0, 0.375 * (north_centre + west))
        above = pltpu.roll(centre, NZ - 1, 0)
        up = jnp.where(layer == NZ - 1, 0.0, ASPECT * 0.5 * (centre + above))
        down = jnp.where(layer == 0, 0.0, pltpu.roll(up, 1, 0))
        coef[LOW, i - 1] = down
        upper[i - 1] = up
        column = (up + down) + jnp.where(layer == 0, fric[i - 1], 0.0)
        coef[INV_U, i - 1] = 4.0 * (face_e + face_w) + (face_n + face_s) + column
        coef[INV_V, i - 1] = face_e + face_w + 4.0 * (face_n + face_s) + column
        return carry

    lax.fori_loop(1, ROWS + 1, row, 0)
    inside = visc[pl.ds(1, ROWS), 0, :] > 0.0
    ratio_u = ratio_v = None
    for layer_index in range(NZ):
        pivot_u = coef[INV_U, :, layer_index, :]
        pivot_v = coef[INV_V, :, layer_index, :]
        if layer_index > 0:
            low = coef[LOW, :, layer_index, :]
            pivot_u = pivot_u - low * ratio_u
            pivot_v = pivot_v - low * ratio_v
        inverse_u = jnp.where(inside, 1.0 / pivot_u, 0.0)
        inverse_v = jnp.where(inside, 1.0 / pivot_v, 0.0)
        up = upper[:, layer_index, :]
        ratio_u = up * inverse_u
        ratio_v = up * inverse_v
        coef[INV_U, :, layer_index, :] = inverse_u
        coef[INV_V, :, layer_index, :] = inverse_v
        coef[Q_U, :, layer_index, :] = ratio_u
        coef[Q_V, :, layer_index, :] = ratio_v


def run_sweeps(coef, load, fields, load_layer, finish):
    far = NZ - 1 if load_layer == 0 else 0

    def take(which, i, layer_index):
        return jnp.broadcast_to(coef[which, i, layer_index : layer_index + 1, :], (KD, NY))

    def solve(i, right_u, right_v, last):
        forward_u, forward_v = [], []
        for k in range(NZ):
            u, v = right_u(k), right_v(k)
            if k == load_layer:
                u = load[i, 0] if u is None else u + load[i, 0]
                v = load[i, 1] if v is None else v + load[i, 1]
            if k > 0 and forward_u[-1] is not None:
                low = take(LOW, i, k)
                below_u, below_v = low * forward_u[-1], low * forward_v[-1]
                u = below_u if u is None else u + below_u
                v = below_v if v is None else v + below_v
            forward_u.append(None if u is None else u * take(INV_U, i, k))
            forward_v.append(None if v is None else v * take(INV_V, i, k))
        solved_u, solved_v = [None] * NZ, [None] * NZ
        solved_u[-1], solved_v[-1] = forward_u[-1], forward_v[-1]
        if not (last and far == NZ - 1):
            for k in range(NZ - 2, -1, -1):
                u = take(Q_U, i, k) * solved_u[k + 1]
                v = take(Q_V, i, k) * solved_v[k + 1]
                solved_u[k] = u if forward_u[k] is None else forward_u[k] + u
                solved_v[k] = v if forward_v[k] is None else forward_v[k] + v
        return solved_u, solved_v

    for sweep in range(SWEEPS):
        source, target = fields[(sweep + 1) % 2], fields[sweep % 2]
        last = sweep == SWEEPS - 1

        def row(i, carry, sweep=sweep, source=source, target=target, last=last):
            if sweep == 0:
                nothing = lambda k: None
                solved_u, solved_v = solve(i, nothing, nothing, last)
            else:

                def sides(component, k, along):
                    other = 1 - component
                    mine, east, west = (source[i + d, component, k] for d in (0, 1, -1))
                    cross_e, cross_w = (source[i + d, other, k] for d in (1, -1))
                    direct = take(F_E, i, k) * east + take(F_W, i, k) * west
                    if along:
                        direct = 4.0 * direct
                        scaled = mine
                    else:
                        scaled = 4.0 * mine
                    north = take(A_N, i, k) * scaled + (
                        take(C_PP, i, k) * cross_e + take(C_MP, i, k) * cross_w
                    )
                    south = take(A_S, i, k) * scaled + (
                        take(C_PM, i, k) * cross_e + take(C_MM, i, k) * cross_w
                    )
                    return direct + (pltpu.roll(north, NY - 1, 1) + pltpu.roll(south, 1, 1))

                solved_u, solved_v = solve(
                    i,
                    lambda k: sides(0, k, True),
                    lambda k: sides(1, k, False),
                    last,
                )
            if last:
                finish(i - CX, solved_u[far], solved_v[far])
            else:
                for k in range(NZ):
                    target[i, 0, k] = solved_u[k]
                    target[i, 1, k] = solved_v[k]
            return carry

        def pair(j, carry, row=row, sweep=sweep):
            return row(sweep + 2 * j + 1, row(sweep + 2 * j, carry))

        lax.fori_loop(0, ROWS // 2 - sweep, pair, 0)


def sides_of(at):
    odd = lax.rem(at, 2)
    return 2 - 2 * odd, 2 * odd


def state_kernel(
    at_ref, own, swap_a, swap_b, edge_c, edge_d, surface, coef, gain, visc, upper, fric, load, field_a, field_b
):
    at = at_ref[0]
    part_a, part_b = sides_of(at)
    upper_pair = lax.rem(at, 4) // 2
    visc[(ROWS + 1) * (1 - upper_pair)] = edge_c[...]
    visc[(ROWS + 1) * upper_pair] = edge_d[...]
    for part, packed in ((part_a, swap_a), (1, own), (part_b, swap_b)):
        for x in range(CX):
            i = part * CX + x
            visc[i + 1] = packed[V_AT + x * NZ : V_AT + (x + 1) * NZ, :]
            friction = packed[F_AT + x : F_AT + x + 1, :]
            fric[i] = friction
            probes = packed[P_AT + x * KD : P_AT + (x + 1) * KD, :]
            for m in range(2):
                basal = -(friction * packed[B_AT + 2 * x + m : B_AT + 2 * x + m + 1, :])
                if packed is own:
                    gain[m, x : x + 1, :] = basal
                load[i, m] = basal * probes
    build_coefs(visc, fric, coef, upper)

    def finish(x, u, v):
        surface[0, x] = u
        surface[1, x] = v

    run_sweeps(coef, load, (field_a, field_b), 0, finish)


def adjoint_kernel(
    returned, meta, coef, gain, panel_high, panel_low, hessian, moments, load, field_a, field_b
):
    beside = meta[:, 1, :]
    metas = (beside, meta[:, 0, :], pltpu.roll(beside, TILES, 1))
    for part, k in enumerate((1, 0, 2)):
        top = top_load(returned[pl.ds(k, TILES, stride=4), :], metas[part])
        for x in range(CX):
            for m in range(2):
                load[part * CX + x, m] = top[m * KD : (m + 1) * KD, x * NY : (x + 1) * NY]

    def finish(x, u, v):
        hessian[x] = gain[0, pl.ds(x, 1), :] * u + gain[1, pl.ds(x, 1), :] * v

    run_sweeps(coef, load, (field_a, field_b), NZ - 1, finish)
    whole = jnp.concatenate([hessian[x] for x in range(CX)], axis=1)
    moments[...] = dot3(split2(whole), (panel_high[...], panel_low[...]), NT)


def from_tile(value, shift):
    moved = pltpu.roll(value, -shift % TILES, 0)
    edge = TILES - 1 if shift > 0 else 0
    return jnp.where(iota(value.shape, 0) == edge, 0.0, moved)


def gram_kernel(
    me_ref, own, near, across, back, asked, panel_high, panel_low, payload, gram_11, gram_12, gram_22
):
    me = me_ref[0]
    count = own.shape[0] // CX
    for shift, block in enumerate((own, near, across, back)):
        source = me ^ shift
        flat = jnp.concatenate(
            [block[pl.ds(x, count, stride=CX), :] for x in range(CX)], axis=1
        )
        at = pl.ds(pl.multiple_of(source * count, count), count)
        panel_high[at, :], panel_low[at, :] = split2(flat)
    upper = panel_high[0:HALF, :], panel_low[0:HALF, :]
    lower = panel_high[HALF:, :], panel_low[HALF:, :]
    gram_11[...] = dot3(upper, upper, NT)
    gram_12[...] = dot3(upper, lower, NT)
    gram_22[...] = dot3(lower, lower, NT)
    here = asked[...]
    payload[:, 0, :] = here
    payload[:, 1, :] = from_tile(here, -1) + pltpu.roll(from_tile(here, 1), TILES, 1)
    for k, n, block in gram_lines(gram_11, gram_12, gram_22):
        payload[:, k, :] = block[pl.ds(n, TILES, stride=2), :]


def gram_lines(gram_11, gram_12, gram_22):
    return (2, 0, gram_11), (3, 0, gram_12), (4, 1, gram_11), (5, 1, gram_12), (6, 0, gram_22), (7, 1, gram_22)


def small_inverse(p):
    size = len(p)
    if size == 2:
        (a, b), (_, d) = p
        scale = 1.0 / (a * d - b * b)
        off = -b * scale
        return [[d * scale, off], [off, a * scale]]
    h = size // 2

    def times(x, y):
        return [
            [functools.reduce(lambda u, v: u + v, [x[i][k] * y[k][j] for k in range(h)]) for j in range(h)]
            for i in range(h)
        ]

    a = [row[:h] for row in p[:h]]
    b = [row[h:] for row in p[:h]]
    c = [row[:h] for row in p[h:]]
    d = [row[h:] for row in p[h:]]
    a_inv = small_inverse(a)
    x = times(a_inv, b)
    cx = times(c, x)
    s_inv = small_inverse([[d[i][j] - cx[i][j] for j in range(h)] for i in range(h)])
    xs = times(x, s_inv)
    x_t = [[x[j][i] for j in range(h)] for i in range(h)]
    corner = times(xs, x_t)
    top = [
        [a_inv[i][j] + corner[i][j] for j in range(h)] + [-xs[i][j] for j in range(h)]
        for i in range(h)
    ]
    bottom = [[-xs[j][i] for j in range(h)] + s_inv[i] for i in range(h)]
    return top + bottom


def invert_block(block):
    size = block.shape[0]
    row_of = iota(block.shape, 0)
    lane_of = iota(block.shape, 1)
    for k in range(0, size, PIVOTS):
        columns = [jnp.broadcast_to(block[:, k + j : k + j + 1], block.shape) for j in range(PIVOTS)]
        pivots = [[columns[j][k + i : k + i + 1, :] for j in range(PIVOTS)] for i in range(PIVOTS)]
        inverse = small_inverse(pivots)
        own_lane = (lane_of >= k) & (lane_of < k + PIVOTS)
        own = own_lane | ((row_of >= k) & (row_of < k + PIVOTS))
        rows = [
            jnp.where(
                own_lane[0:1, :],
                jnp.where(lane_of[0:1, :] == k + j, 1.0, 0.0),
                block[k + j : k + j + 1, :],
            )
            for j in range(PIVOTS)
        ]
        block = jnp.where(own, 0.0, block)
        in_rows = (row_of >= k) & (row_of < k + PIVOTS)
        for j in range(PIVOTS):
            row = functools.reduce(
                lambda u, v: u + v, [inverse[j][i] * rows[i] for i in range(PIVOTS)]
            )
            column = jnp.where(in_rows, jnp.where(row_of == k + j, -1.0, 0.0), columns[j])
            block = block - column * row
    return block


def dot_f32(a, b):
    a1, a2, a3 = split3(a)
    b1, b2, b3 = split3(b)
    small = dot(a1, b3, NN) + dot(a3, b1, NN) + dot(a2, b2, NN)
    return dot(a1, b1, NN) + ((dot(a1, b2, NN) + dot(a2, b1, NN)) + small)


def eliminate(matrix, number):
    size = matrix.shape[0]
    at = slice(number * BLOCK, (number + 1) * BLOCK)
    inverse = invert_block(matrix[at, at])
    panel = matrix[at, :]
    columns = matrix[:, at]
    lanes = iota((BLOCK, size), 1)
    own_lanes = (lanes >= number * BLOCK) & (lanes < (number + 1) * BLOCK)
    identity = (iota((BLOCK, size), 0) + number * BLOCK == lanes).astype(f32)
    rows = dot_f32(inverse, jnp.where(own_lanes, identity, panel))
    rest = matrix[...]
    all_lanes = iota((size, size), 1)
    inside = (all_lanes >= number * BLOCK) & (all_lanes < (number + 1) * BLOCK)
    matrix[...] = jnp.where(inside, 0.0, rest) - dot_f32(columns, rows)
    matrix[at, :] = rows


def first_kernel(arrived, matrix, gram_11, gram_12, gram_22):
    for k, n, block in gram_lines(gram_11, gram_12, gram_22):
        block[pl.ds(n, TILES, stride=2), :] = arrived[:, k, :]
    matrix[0:HALF, 0:HALF] = gram_11[...]
    matrix[0:HALF, HALF:] = gram_12[...]
    matrix[HALF:, 0:HALF] = jnp.transpose(gram_12[...])
    matrix[HALF:, HALF:] = gram_22[...]
    eliminate(matrix, 0)


def next_kernel(number, before, matrix):
    matrix[...] = before[...]
    eliminate(matrix, number)


def slot_rows(meta):
    wide = jnp.concatenate([meta, jnp.zeros((128 - TILES, 128), f32)], axis=0)
    turned = jnp.transpose(wide)
    half = CAP // 2

    def paired(at):
        return turned[at : at + half] + pltpu.roll(turned[at + half : at + CAP], TILES, 1)

    return paired(0), paired(CAP), paired(2 * CAP)


def slot_one_hot(cells):
    index = cells.astype(jnp.int32)
    at = iota((CX * NY, 128), 0)
    return jnp.concatenate(
        [(at == index[j : j + 1, :]).astype(f32).astype(bf16) for j in range(CAP // 2)], axis=1
    )


def gather_kernel(meta, surface, payload):
    cells, sight_u, sight_v = slot_rows(meta[:, 0, :])
    one_hot = slot_one_hot(cells)
    both = jnp.concatenate(
        [jnp.concatenate([surface[m, x] for x in range(CX)], axis=1) for m in range(2)], axis=0
    )
    picked = dot(jnp.concatenate(split3(both), axis=0), one_hot, NN)
    n = 2 * KD
    picked = picked[0:n] + (picked[n : 2 * n] + picked[2 * n : 3 * n])
    chunks = []
    for j in range(CAP // 2):
        at = slice(j * 128, (j + 1) * 128)
        chunks.append(
            sight_u[j : j + 1, :] * picked[0:KD, at] + sight_v[j : j + 1, :] * picked[KD:n, at]
        )
    chunks.append(jnp.zeros((128 - TILES, 128), f32))
    turned = jnp.transpose(jnp.concatenate(chunks, axis=0))
    payload[...] = jnp.broadcast_to(jnp.sum(meta[...], axis=0, keepdims=True), payload.shape)
    payload[:, 0, :] = turned[0:TILES] + pltpu.roll(turned[TILES:], TILES, 1)


def split_kernel(precision, high, low):
    high[...], low[...] = split2(precision[...])


def precision_kernel(arrived, slots, precision_high, precision_low, payload):
    rows = precision_high.shape[0]

    one_hot = (iota((128, rows), 0) == slots[0:1, :]).astype(f32).astype(bf16)
    rank = slots[1:2, :]
    mine = arrived[:, 0, :]
    turned = jnp.transpose(jnp.concatenate([mine, jnp.zeros((128 - TILES, 128), f32)], axis=0))
    spread = [dot(part, one_hot, NN) for part in split3(turned)]
    spread = spread[0] + (spread[1] + spread[2])
    predicted = jnp.zeros((KD, rows), f32)
    for s in range(CAP):
        predicted = predicted + jnp.where(rank == s, spread[s * KD : (s + 1) * KD], 0.0)
    weighted = dot3(split2(predicted), (precision_high[...], precision_low[...]), NN)
    spots = jnp.concatenate([jnp.where(rank == s, weighted, 0.0) for s in range(CAP)], axis=0)
    sent = [dot(one_hot, part, NT) for part in split3(spots)]
    sent = sent[0] + (sent[1] + sent[2])
    sent = sent[0:TILES]
    payload[pl.ds(0, TILES, stride=4), :] = sent
    payload[pl.ds(1, TILES, stride=4), :] = from_tile(sent, -1)
    payload[pl.ds(2, TILES, stride=4), :] = from_tile(sent, 1)
    payload[pl.ds(3, TILES, stride=4), :] = jnp.zeros((TILES, 128), f32)


def top_load(mine, meta):
    cells, *sights = slot_rows(meta)
    one_hot = slot_one_hot(cells)
    turned = jnp.transpose(jnp.concatenate([mine, pltpu.roll(mine, TILES, 1)], axis=0))
    loads = []
    for m in range(2):
        loads.append(
            jnp.concatenate(
                [turned[j * KD : (j + 1) * KD] * sights[m][j : j + 1, :] for j in range(CAP // 2)],
                axis=1,
            )
        )
    parts = dot(jnp.concatenate(split3(jnp.concatenate(loads, axis=0)), axis=0), one_hot, NT)
    n = 2 * KD
    return parts[0:n] + (parts[n : 2 * n] + parts[2 * n : 3 * n])


def copies_kernel(own, other, copies):
    copies[...] = jnp.broadcast_to((own[...] + other[...])[None], copies.shape)


def last_kernel(number, before, panel_high, panel_low, high, middle, low, spread_high, spread_low, matrix):
    matrix[...] = before[...]
    eliminate(matrix, number)
    inverse = matrix[...]
    high[...], middle[...], low[...] = split3(inverse)
    spread = dot3(split2(inverse), (panel_high[...], panel_low[...]), NN)
    spread_high[...], spread_low[...] = split2(spread)


def final_kernel(parts, high, middle, low, spread_high, spread_low, hessian, filtered, coefficients):
    a1, a2, a3 = split3(jnp.sum(parts[...], axis=0))
    removed = dot3((a1, a2), (spread_high[...], spread_low[...]), NN)
    b1, b2, b3 = high[...], middle[...], low[...]
    small = dot(a1, b3, NN) + dot(a3, b1, NN) + dot(a2, b2, NN)
    coefficients[...] = dot(a1, b1, NN) + ((dot(a1, b2, NN) + dot(a2, b1, NN)) + small)
    for x in range(CX):
        filtered[x] = hessian[x] - removed[:, x * NY : (x + 1) * NY]


def swap(value, axis, distance, offset=0):
    count = lax.axis_size(axis)
    partner = [((i + offset) ^ distance) - offset for i in range(count)]
    return lax.ppermute(value, axis, [(i, j) for i, j in enumerate(partner) if 0 <= j < count])


def per_device(
    probes, viscosity, friction, base_velocity, obs_tile, obs_cell, sight_lines, obs_precision, basis
):
    cells = CX * NY
    me = lax.axis_index("probe").astype(jnp.int32).reshape(1)
    at = lax.axis_index("tile").astype(jnp.int32).reshape(1)
    rows = obs_cell.shape[0]
    arguments = [
        viscosity.reshape(CX * NZ, NY),
        probes.reshape(CX * KD, NY),
        base_velocity.reshape(CX * 2, NY),
        friction,
    ]
    others = [swap(basis.reshape(-1, NY), "probe", d) for d in (1, 2, 3)]
    packed, edge_c, edge_d = call(
        prepare_kernel,
        [sds((PACK, NY)), sds((NZ, NY)), sds((NZ, NY))],
        [at, *arguments],
        places=[SM] + [pl.BlockSpec(memory_space=pltpu.HBM)] * len(arguments),
        scratch=[pltpu.VMEM((CX, NY), f32), pltpu.SemaphoreType.DMA((6,))],
        moved=400000,
        vmem=VMEM_PREP,
    )
    asked, slots, own_basis = call(
        meta_kernel,
        [sds((TILES, 128)), sds((2, rows), jnp.int32), sds((basis.shape[0] * CX, NY))],
        [obs_tile.reshape(1, -1), obs_cell.reshape(1, -1), sight_lines, basis.reshape(-1, NY)],
        flops=10**10,
        moved=400000,
    )
    swap_a = swap(packed, "tile", 1)
    swap_b = swap(packed, "tile", 1, 1)
    far_c = swap(edge_c, "tile", 2)
    far_d = swap(edge_d, "tile", 2, 2)
    asked, swap_b, far_c, far_d = lax.optimization_barrier((asked, swap_b, far_c, far_d))
    n_basis = 4 * basis.shape[0]
    panel_high, panel_low, request = call(
        gram_kernel,
        [sds((n_basis, cells), bf16), sds((n_basis, cells), bf16), sds((TILES, 8, 128))],
        [me, own_basis, *others, asked],
        scratch=[pltpu.VMEM((HALF, HALF), f32)] * 3,
        scalars=1,
        flops=20 * 10**9,
        moved=1500000,
    )

    def exchange(value):
        return lax.all_to_all(value, "tile", split_axis=0, concat_axis=0, tiled=True)

    meta = exchange(request)
    precision_parts = call(
        split_kernel,
        [sds(obs_precision.shape, bf16), sds(obs_precision.shape, bf16)],
        [obs_precision],
        flops=2 * 10**9,
        moved=2000000,
    )
    precision_parts, meta = lax.optimization_barrier((precision_parts, meta))

    field = pltpu.VMEM((ROWS, 2, NZ, KD, NY), f32)
    load = pltpu.VMEM((ROWS, 2, KD, NY), f32)
    surface, coef, gain = call(
        state_kernel,
        [sds((2, CX, KD, NY)), sds((N_COEF, ROWS, NZ, NY)), sds((2, CX, NY))],
        [at, packed, swap_a, swap_b, far_c, far_d],
        scalars=1,
        scratch=[
            pltpu.VMEM((ROWS + 2, NZ, NY), f32),
            pltpu.VMEM((ROWS, NZ, NY), f32),
            pltpu.VMEM((ROWS, 1, NY), f32),
            load,
            field,
            field,
        ],
        flops=40 * 16 * 44 * 1024,
        moved=2000000,
    )
    payload = call(
        gather_kernel,
        sds((TILES, 8, 128)),
        [meta, surface],
        flops=2 * 48 * 512 * 1024,
        moved=300000,
    )
    arrived = exchange(payload)
    outgoing = call(
        precision_kernel,
        sds((TILES * 4, 128)),
        [arrived, slots, *precision_parts],
        flops=20 * 10**9,
        moved=1500000,
    )
    returned = exchange(outgoing.reshape(TILES, 4, 128)).reshape(TILES * 4, 128)
    matrix = call(
        first_kernel,
        sds((n_basis, n_basis)),
        [arrived],
        scratch=[pltpu.VMEM((HALF, HALF), f32)] * 3,
        flops=12 * 64 * 256 * 256,
        moved=500000,
    )
    number = 1

    def invert(matrix, pieces):
        nonlocal number
        for _ in range(pieces):
            matrix = call(
                functools.partial(next_kernel, number),
                sds((n_basis, n_basis)),
                [matrix],
                flops=12 * 64 * 256 * 256,
                moved=500000,
            )
            number += 1
        return matrix

    matrix = invert(matrix, PIECES[0])
    returned, matrix = lax.optimization_barrier((returned, matrix))
    hessian, moments = call(
        adjoint_kernel,
        [sds((CX, KD, NY)), sds((KD, n_basis))],
        [returned, meta, coef, gain, panel_high, panel_low],
        scratch=[load, field, field],
        flops=40 * 16 * 44 * 1024,
        moved=2000000,
    )
    moments, matrix = lax.optimization_barrier((moments, matrix))
    half = TILES // 2
    copies = call(
        copies_kernel,
        sds((half, KD, n_basis)),
        [moments, swap(moments, "tile", 1)],
        flops=half * KD * n_basis,
        moved=4 * half * KD * n_basis,
    )
    parts = lax.all_to_all(
        copies,
        "tile",
        split_axis=0,
        concat_axis=0,
        tiled=True,
        axis_index_groups=[list(range(core, TILES, 2)) for core in range(2)],
    )
    matrix = invert(matrix, PIECES[1])
    inverse = call(
        functools.partial(last_kernel, number),
        [sds((n_basis, n_basis), bf16)] * 3 + [sds((n_basis, cells), bf16)] * 2,
        [matrix, panel_high, panel_low],
        scratch=[pltpu.VMEM((n_basis, n_basis), f32)],
        flops=12 * 64 * 256 * 256 + 6 * 256 * 256 * 512,
        moved=1500000,
    )
    filtered, coefficients = call(
        final_kernel,
        [sds((CX, KD, NY)), sds((KD, n_basis))],
        [parts, *inverse, hessian],
        flops=12 * 8 * 256 * 512,
        moved=800000,
    )
    return filtered, coefficients


def solution(mesh):
    in_specs = (
        P("tile", "probe", None),
        P("tile", None, None),
        P("tile", None),
        P("tile", None, None),
        P("tile", None),
        P("tile"),
        P(None, "tile"),
        P("tile", None),
        P("probe", "tile", None),
    )
    out_specs = (P("tile", "probe", None), P("probe", None))
    return jax.shard_map(
        per_device, mesh=mesh, in_specs=in_specs, out_specs=out_specs, check_vma=False
    )
```

```python
import functools

import jax
import jax.numpy as jnp
from jax import lax
from jax.experimental import pallas as pl
from jax.experimental.pallas import tpu as pltpu
from jax.sharding import PartitionSpec as P

SWEEPS = 5
CX = 4
NY = 128
NZ = 16
KD = 8
CAP = 16
HALF = 128
TILES = 64
ROWS = CX * 3
ASPECT = 1024.0
N_COEF = 13
F_E, F_W, A_N, A_S, C_PP, C_MP, C_PM, C_MM, LOW, INV_U, INV_V, Q_U, Q_V = range(N_COEF)
BLOCK = 32
VMEM_PREP = 60
PIVOTS = 4
PIECES = (3, 3)
V_AT, P_AT, B_AT, F_AT = 0, CX * NZ, CX * (NZ + KD), CX * (NZ + KD + 2)
O_AT, PACK = F_AT + 4, F_AT + 24
f32 = jnp.float32
bf16 = jnp.bfloat16
VM = pl.BlockSpec(memory_space=pltpu.VMEM)
SM = pl.BlockSpec(memory_space=pltpu.SMEM)

NN = (((1,), (0,)), ((), ()))
NT = (((1,), (1,)), ((), ()))


def call(kernel, out_shape, args, scratch=(), scalars=0, flops=0, moved=0, places=None, vmem=14):
    single = not isinstance(out_shape, (list, tuple))
    shapes = [out_shape] if single else list(out_shape)
    out = pl.pallas_call(
        kernel,
        out_shape=shapes,
        in_specs=places or [SM] * scalars + [VM] * (len(args) - scalars),
        out_specs=[VM] * len(shapes),
        scratch_shapes=list(scratch),
        compiler_params=pltpu.CompilerParams(vmem_limit_bytes=int(vmem * 2**20)),
        cost_estimate=pl.CostEstimate(flops=flops, bytes_accessed=moved, transcendentals=0),
    )(*args)
    return out[0] if single else out


def sds(shape, dtype=f32):
    return jax.ShapeDtypeStruct(shape, dtype)


def dot(a, b, dims):
    return lax.dot_general(a, b, dims, preferred_element_type=f32)


def split2(x):
    high = x.astype(bf16)
    return high, (x - high.astype(f32)).astype(bf16)


def split3(x):
    high = x.astype(bf16)
    rest = x - high.astype(f32)
    middle = rest.astype(bf16)
    return high, middle, (rest - middle.astype(f32)).astype(bf16)


def dot3(a, b, dims):
    a_high, a_low = a
    b_high, b_low = b
    return dot(a_high, b_high, dims) + (dot(a_high, b_low, dims) + dot(a_low, b_high, dims))


def iota(shape, axis):
    return lax.broadcasted_iota(jnp.int32, shape, axis)


def prepare_kernel(
    at_ref, visc, probes, base, fric, tile_row, cell_row, sight,
    packed, edge_c, edge_d, fric_in, tile_in, cell_in, sight_in, sems,
):
    upper_pair = lax.rem(at_ref[0], 4) // 2
    high_row = pl.multiple_of((CX - 1) * NZ * (1 - upper_pair), NZ)
    low_row = pl.multiple_of((CX - 1) * NZ * upper_pair, NZ)
    moves = [
        (fric, fric_in),
        (tile_row, tile_in),
        (cell_row, cell_in),
        (sight, sight_in),
        (visc, packed.at[pl.ds(V_AT, CX * NZ), :]),
        (probes, packed.at[pl.ds(P_AT, CX * KD), :]),
        (base, packed.at[pl.ds(B_AT, CX * 2), :]),
        (visc.at[pl.ds(high_row, NZ), :], edge_c),
        (visc.at[pl.ds(low_row, NZ), :], edge_d),
    ]
    copies = [
        pltpu.make_async_copy(source, target, sems.at[n])
        for n, (source, target) in enumerate(moves)
    ]
    for copy in copies:
        copy.start()
    for copy in copies:
        copy.wait()
    tail = [fric_in[...]]
    for line in (tile_in[...], cell_in[...], sight_in[0:1, :], sight_in[1:2, :]):
        tail += [line[:, n : n + 128].astype(f32) for n in range(0, line.shape[1], 128)]
    tail.append(jnp.zeros((4, NY), f32))
    packed[F_AT:PACK, :] = jnp.concatenate(tail, axis=0)


def meta_kernel(packed, basis, asked, slots, own_basis):
    own_basis[...] = basis[...]
    rows = slots.shape[1]

    def line(at):
        start = O_AT + at * (rows // 128)
        return jnp.concatenate(
            [packed[n : n + 1, :] for n in range(start, start + rows // 128)], axis=1
        )

    tiles = line(0).astype(jnp.int32)
    one_hot = (iota((TILES, rows), 0) == tiles).astype(f32)
    before = (iota((rows, rows), 0) < iota((rows, rows), 1)).astype(f32).astype(bf16)
    one_hot_b = one_hot.astype(bf16)
    earlier = dot(one_hot_b, before, NN)
    rank = jnp.sum(one_hot * earlier, axis=0, keepdims=True).astype(jnp.int32)
    slots[0:1, :] = tiles
    slots[1:2, :] = rank
    chosen = (iota((CAP, rows), 0) == rank).astype(f32)
    values = jnp.concatenate(
        [
            chosen * line(1),
            chosen * line(2),
            chosen * line(3),
            jnp.zeros((128 - 3 * CAP, rows), f32),
        ],
        axis=0,
    )
    parts = [dot(one_hot_b, part, NT) for part in split3(values)]
    asked[...] = parts[0] + (parts[1] + parts[2])


def build_coefs(visc, fric, coef, upper):
    lane = iota((NZ, NY), 1)
    layer = iota((NZ, NY), 0)

    def row(i, carry):
        centre = visc[i]
        east = visc[i + 1]
        west = visc[i - 1]

        def from_south(x):
            return pltpu.roll(x, 1, 1)

        def from_north(x):
            return pltpu.roll(x, NY - 1, 1)

        south_centre = jnp.where(lane == 0, 0.0, from_south(centre))
        north_centre = jnp.where(lane == NY - 1, 0.0, from_north(centre))
        face_e = 0.5 * (centre + east)
        face_w = 0.5 * (centre + west)
        face_n = 0.5 * (centre + north_centre)
        face_s = 0.5 * (centre + south_centre)
        coef[F_E, i - 1] = face_e
        coef[F_W, i - 1] = face_w
        coef[A_N, i - 1] = jnp.where(lane == 0, 0.0, face_s)
        coef[A_S, i - 1] = jnp.where(lane == NY - 1, 0.0, face_n)
        coef[C_PP, i - 1] = jnp.where(lane == 0, 0.0, 0.375 * (south_centre + east))
        coef[C_MP, i - 1] = jnp.where(lane == 0, 0.0, -0.375 * (south_centre + west))
        coef[C_PM, i - 1] = jnp.where(lane == NY - 1, 0.0, -0.375 * (north_centre + east))
        coef[C_MM, i - 1] = jnp.where(lane == NY - 1, 0.0, 0.375 * (north_centre + west))
        above = pltpu.roll(centre, NZ - 1, 0)
        up = jnp.where(layer == NZ - 1, 0.0, ASPECT * 0.5 * (centre + above))
        down = jnp.where(layer == 0, 0.0, pltpu.roll(up, 1, 0))
        coef[LOW, i - 1] = down
        upper[i - 1] = up
        column = (up + down) + jnp.where(layer == 0, fric[i - 1], 0.0)
        coef[INV_U, i - 1] = 4.0 * (face_e + face_w) + (face_n + face_s) + column
        coef[INV_V, i - 1] = face_e + face_w + 4.0 * (face_n + face_s) + column
        return carry

    lax.fori_loop(1, ROWS + 1, row, 0)
    inside = visc[pl.ds(1, ROWS), 0, :] > 0.0
    ratio_u = ratio_v = None
    for layer_index in range(NZ):
        pivot_u = coef[INV_U, :, layer_index, :]
        pivot_v = coef[INV_V, :, layer_index, :]
        if layer_index > 0:
            low = coef[LOW, :, layer_index, :]
            pivot_u = pivot_u - low * ratio_u
            pivot_v = pivot_v - low * ratio_v
        inverse_u = jnp.where(inside, 1.0 / pivot_u, 0.0)
        inverse_v = jnp.where(inside, 1.0 / pivot_v, 0.0)
        up = upper[:, layer_index, :]
        ratio_u = up * inverse_u
        ratio_v = up * inverse_v
        coef[INV_U, :, layer_index, :] = inverse_u
        coef[INV_V, :, layer_index, :] = inverse_v
        coef[Q_U, :, layer_index, :] = ratio_u
        coef[Q_V, :, layer_index, :] = ratio_v


def run_sweeps(coef, load, fields, load_layer, finish):
    far = NZ - 1 if load_layer == 0 else 0

    def take(which, i, layer_index):
        return jnp.broadcast_to(coef[which, i, layer_index : layer_index + 1, :], (KD, NY))

    def solve(i, right_u, right_v, last):
        forward_u, forward_v = [], []
        for k in range(NZ):
            u, v = right_u(k), right_v(k)
            if k == load_layer:
                u = load[i, 0] if u is None else u + load[i, 0]
                v = load[i, 1] if v is None else v + load[i, 1]
            if k > 0 and forward_u[-1] is not None:
                low = take(LOW, i, k)
                below_u, below_v = low * forward_u[-1], low * forward_v[-1]
                u = below_u if u is None else u + below_u
                v = below_v if v is None else v + below_v
            forward_u.append(None if u is None else u * take(INV_U, i, k))
            forward_v.append(None if v is None else v * take(INV_V, i, k))
        solved_u, solved_v = [None] * NZ, [None] * NZ
        solved_u[-1], solved_v[-1] = forward_u[-1], forward_v[-1]
        if not (last and far == NZ - 1):
            for k in range(NZ - 2, -1, -1):
                u = take(Q_U, i, k) * solved_u[k + 1]
                v = take(Q_V, i, k) * solved_v[k + 1]
                solved_u[k] = u if forward_u[k] is None else forward_u[k] + u
                solved_v[k] = v if forward_v[k] is None else forward_v[k] + v
        return solved_u, solved_v

    for sweep in range(SWEEPS):
        source, target = fields[(sweep + 1) % 2], fields[sweep % 2]
        last = sweep == SWEEPS - 1

        def row(i, carry, sweep=sweep, source=source, target=target, last=last):
            if sweep == 0:
                nothing = lambda k: None
                solved_u, solved_v = solve(i, nothing, nothing, last)
            else:

                def sides(component, k, along):
                    other = 1 - component
                    mine, east, west = (source[i + d, component, k] for d in (0, 1, -1))
                    cross_e, cross_w = (source[i + d, other, k] for d in (1, -1))
                    direct = take(F_E, i, k) * east + take(F_W, i, k) * west
                    if along:
                        direct = 4.0 * direct
                        scaled = mine
                    else:
                        scaled = 4.0 * mine
                    north = take(A_N, i, k) * scaled + (
                        take(C_PP, i, k) * cross_e + take(C_MP, i, k) * cross_w
                    )
                    south = take(A_S, i, k) * scaled + (
                        take(C_PM, i, k) * cross_e + take(C_MM, i, k) * cross_w
                    )
                    return direct + (pltpu.roll(north, NY - 1, 1) + pltpu.roll(south, 1, 1))

                solved_u, solved_v = solve(
                    i,
                    lambda k: sides(0, k, True),
                    lambda k: sides(1, k, False),
                    last,
                )
            if last:
                finish(i - CX, solved_u[far], solved_v[far])
            else:
                for k in range(NZ):
                    target[i, 0, k] = solved_u[k]
                    target[i, 1, k] = solved_v[k]
            return carry

        def pair(j, carry, row=row, sweep=sweep):
            return row(sweep + 2 * j + 1, row(sweep + 2 * j, carry))

        lax.fori_loop(0, ROWS // 2 - sweep, pair, 0)


def sides_of(at):
    odd = lax.rem(at, 2)
    return 2 - 2 * odd, 2 * odd


def state_kernel(
    at_ref, own, swap_a, swap_b, edge_c, edge_d, surface, coef, gain, visc, upper, fric, load, field_a, field_b
):
    at = at_ref[0]
    part_a, part_b = sides_of(at)
    upper_pair = lax.rem(at, 4) // 2
    visc[(ROWS + 1) * (1 - upper_pair)] = edge_c[...]
    visc[(ROWS + 1) * upper_pair] = edge_d[...]
    for part, packed in ((part_a, swap_a), (1, own), (part_b, swap_b)):
        for x in range(CX):
            i = part * CX + x
            visc[i + 1] = packed[V_AT + x * NZ : V_AT + (x + 1) * NZ, :]
            friction = packed[F_AT + x : F_AT + x + 1, :]
            fric[i] = friction
            probes = packed[P_AT + x * KD : P_AT + (x + 1) * KD, :]
            for m in range(2):
                basal = -(friction * packed[B_AT + 2 * x + m : B_AT + 2 * x + m + 1, :])
                if packed is own:
                    gain[m, x : x + 1, :] = basal
                load[i, m] = basal * probes
    build_coefs(visc, fric, coef, upper)

    def finish(x, u, v):
        surface[0, x] = u
        surface[1, x] = v

    run_sweeps(coef, load, (field_a, field_b), 0, finish)


def adjoint_kernel(
    returned, meta, coef, gain, panel_high, panel_low, hessian, moments, load, field_a, field_b
):
    beside = meta[:, 1, :]
    metas = (beside, meta[:, 0, :], pltpu.roll(beside, TILES, 1))
    for part, k in enumerate((1, 0, 2)):
        top = top_load(returned[pl.ds(k, TILES, stride=4), :], metas[part])
        for x in range(CX):
            for m in range(2):
                load[part * CX + x, m] = top[m * KD : (m + 1) * KD, x * NY : (x + 1) * NY]

    def finish(x, u, v):
        hessian[x] = gain[0, pl.ds(x, 1), :] * u + gain[1, pl.ds(x, 1), :] * v

    run_sweeps(coef, load, (field_a, field_b), NZ - 1, finish)
    whole = jnp.concatenate([hessian[x] for x in range(CX)], axis=1)
    moments[...] = dot3(split2(whole), (panel_high[...], panel_low[...]), NT)


def from_tile(value, shift):
    moved = pltpu.roll(value, -shift % TILES, 0)
    edge = TILES - 1 if shift > 0 else 0
    return jnp.where(iota(value.shape, 0) == edge, 0.0, moved)


def gram_kernel(
    me_ref, own, near, across, back, asked, panel_high, panel_low, payload, gram_11, gram_12, gram_22
):
    me = me_ref[0]
    count = own.shape[0] // CX
    for shift, block in enumerate((own, near, across, back)):
        source = me ^ shift
        flat = jnp.concatenate(
            [block[pl.ds(x, count, stride=CX), :] for x in range(CX)], axis=1
        )
        at = pl.ds(pl.multiple_of(source * count, count), count)
        panel_high[at, :], panel_low[at, :] = split2(flat)
    upper = panel_high[0:HALF, :], panel_low[0:HALF, :]
    lower = panel_high[HALF:, :], panel_low[HALF:, :]
    gram_11[...] = dot3(upper, upper, NT)
    gram_12[...] = dot3(upper, lower, NT)
    gram_22[...] = dot3(lower, lower, NT)
    here = asked[...]
    payload[:, 0, :] = here
    payload[:, 1, :] = from_tile(here, -1) + pltpu.roll(from_tile(here, 1), TILES, 1)
    for k, n, block in gram_lines(gram_11, gram_12, gram_22):
        payload[:, k, :] = block[pl.ds(n, TILES, stride=2), :]


def gram_lines(gram_11, gram_12, gram_22):
    return (2, 0, gram_11), (3, 0, gram_12), (4, 1, gram_11), (5, 1, gram_12), (6, 0, gram_22), (7, 1, gram_22)


def small_inverse(p):
    size = len(p)
    if size == 2:
        (a, b), (_, d) = p
        scale = 1.0 / (a * d - b * b)
        off = -b * scale
        return [[d * scale, off], [off, a * scale]]
    h = size // 2

    def times(x, y):
        return [
            [functools.reduce(lambda u, v: u + v, [x[i][k] * y[k][j] for k in range(h)]) for j in range(h)]
            for i in range(h)
        ]

    a = [row[:h] for row in p[:h]]
    b = [row[h:] for row in p[:h]]
    c = [row[:h] for row in p[h:]]
    d = [row[h:] for row in p[h:]]
    a_inv = small_inverse(a)
    x = times(a_inv, b)
    cx = times(c, x)
    s_inv = small_inverse([[d[i][j] - cx[i][j] for j in range(h)] for i in range(h)])
    xs = times(x, s_inv)
    x_t = [[x[j][i] for j in range(h)] for i in range(h)]
    corner = times(xs, x_t)
    top = [
        [a_inv[i][j] + corner[i][j] for j in range(h)] + [-xs[i][j] for j in range(h)]
        for i in range(h)
    ]
    bottom = [[-xs[j][i] for j in range(h)] + s_inv[i] for i in range(h)]
    return top + bottom


def invert_block(block):
    size = block.shape[0]
    row_of = iota(block.shape, 0)
    lane_of = iota(block.shape, 1)
    for k in range(0, size, PIVOTS):
        columns = [jnp.broadcast_to(block[:, k + j : k + j + 1], block.shape) for j in range(PIVOTS)]
        pivots = [[columns[j][k + i : k + i + 1, :] for j in range(PIVOTS)] for i in range(PIVOTS)]
        inverse = small_inverse(pivots)
        own_lane = (lane_of >= k) & (lane_of < k + PIVOTS)
        own = own_lane | ((row_of >= k) & (row_of < k + PIVOTS))
        rows = [
            jnp.where(
                own_lane[0:1, :],
                jnp.where(lane_of[0:1, :] == k + j, 1.0, 0.0),
                block[k + j : k + j + 1, :],
            )
            for j in range(PIVOTS)
        ]
        block = jnp.where(own, 0.0, block)
        in_rows = (row_of >= k) & (row_of < k + PIVOTS)
        for j in range(PIVOTS):
            row = functools.reduce(
                lambda u, v: u + v, [inverse[j][i] * rows[i] for i in range(PIVOTS)]
            )
            column = jnp.where(in_rows, jnp.where(row_of == k + j, -1.0, 0.0), columns[j])
            block = block - column * row
    return block


def dot_f32(a, b):
    a1, a2, a3 = split3(a)
    b1, b2, b3 = split3(b)
    small = dot(a1, b3, NN) + dot(a3, b1, NN) + dot(a2, b2, NN)
    return dot(a1, b1, NN) + ((dot(a1, b2, NN) + dot(a2, b1, NN)) + small)


def eliminate(matrix, number):
    size = matrix.shape[0]
    at = slice(number * BLOCK, (number + 1) * BLOCK)
    inverse = invert_block(matrix[at, at])
    panel = matrix[at, :]
    columns = matrix[:, at]
    lanes = iota((BLOCK, size), 1)
    own_lanes = (lanes >= number * BLOCK) & (lanes < (number + 1) * BLOCK)
    identity = (iota((BLOCK, size), 0) + number * BLOCK == lanes).astype(f32)
    rows = dot_f32(inverse, jnp.where(own_lanes, identity, panel))
    rest = matrix[...]
    all_lanes = iota((size, size), 1)
    inside = (all_lanes >= number * BLOCK) & (all_lanes < (number + 1) * BLOCK)
    matrix[...] = jnp.where(inside, 0.0, rest) - dot_f32(columns, rows)
    matrix[at, :] = rows


def first_kernel(arrived, matrix, gram_11, gram_12, gram_22):
    for k, n, block in gram_lines(gram_11, gram_12, gram_22):
        block[pl.ds(n, TILES, stride=2), :] = arrived[:, k, :]
    matrix[0:HALF, 0:HALF] = gram_11[...]
    matrix[0:HALF, HALF:] = gram_12[...]
    matrix[HALF:, 0:HALF] = jnp.transpose(gram_12[...])
    matrix[HALF:, HALF:] = gram_22[...]
    eliminate(matrix, 0)


def next_kernel(number, before, matrix):
    matrix[...] = before[...]
    eliminate(matrix, number)


def slot_rows(meta):
    wide = jnp.concatenate([meta, jnp.zeros((128 - TILES, 128), f32)], axis=0)
    turned = jnp.transpose(wide)
    half = CAP // 2

    def paired(at):
        return turned[at : at + half] + pltpu.roll(turned[at + half : at + CAP], TILES, 1)

    return paired(0), paired(CAP), paired(2 * CAP)


def slot_one_hot(cells):
    index = cells.astype(jnp.int32)
    at = iota((CX * NY, 128), 0)
    return jnp.concatenate(
        [(at == index[j : j + 1, :]).astype(f32).astype(bf16) for j in range(CAP // 2)], axis=1
    )


def gather_kernel(meta, surface, payload):
    cells, sight_u, sight_v = slot_rows(meta[:, 0, :])
    one_hot = slot_one_hot(cells)
    both = jnp.concatenate(
        [jnp.concatenate([surface[m, x] for x in range(CX)], axis=1) for m in range(2)], axis=0
    )
    picked = dot(jnp.concatenate(split3(both), axis=0), one_hot, NN)
    n = 2 * KD
    picked = picked[0:n] + (picked[n : 2 * n] + picked[2 * n : 3 * n])
    chunks = []
    for j in range(CAP // 2):
        at = slice(j * 128, (j + 1) * 128)
        chunks.append(
            sight_u[j : j + 1, :] * picked[0:KD, at] + sight_v[j : j + 1, :] * picked[KD:n, at]
        )
    chunks.append(jnp.zeros((128 - TILES, 128), f32))
    turned = jnp.transpose(jnp.concatenate(chunks, axis=0))
    payload[...] = jnp.broadcast_to(jnp.sum(meta[...], axis=0, keepdims=True), payload.shape)
    payload[:, 0, :] = turned[0:TILES] + pltpu.roll(turned[TILES:], TILES, 1)


def split_kernel(precision, high, low):
    high[...], low[...] = split2(precision[...])


def precision_kernel(arrived, slots, precision_high, precision_low, payload):
    rows = precision_high.shape[0]

    one_hot = (iota((128, rows), 0) == slots[0:1, :]).astype(f32).astype(bf16)
    rank = slots[1:2, :]
    mine = arrived[:, 0, :]
    turned = jnp.transpose(jnp.concatenate([mine, jnp.zeros((128 - TILES, 128), f32)], axis=0))
    spread = [dot(part, one_hot, NN) for part in split3(turned)]
    spread = spread[0] + (spread[1] + spread[2])
    predicted = jnp.zeros((KD, rows), f32)
    for s in range(CAP):
        predicted = predicted + jnp.where(rank == s, spread[s * KD : (s + 1) * KD], 0.0)
    weighted = dot3(split2(predicted), (precision_high[...], precision_low[...]), NN)
    spots = jnp.concatenate([jnp.where(rank == s, weighted, 0.0) for s in range(CAP)], axis=0)
    sent = [dot(one_hot, part, NT) for part in split3(spots)]
    sent = sent[0] + (sent[1] + sent[2])
    sent = sent[0:TILES]
    payload[pl.ds(0, TILES, stride=4), :] = sent
    payload[pl.ds(1, TILES, stride=4), :] = from_tile(sent, -1)
    payload[pl.ds(2, TILES, stride=4), :] = from_tile(sent, 1)
    payload[pl.ds(3, TILES, stride=4), :] = jnp.zeros((TILES, 128), f32)


def top_load(mine, meta):
    cells, *sights = slot_rows(meta)
    one_hot = slot_one_hot(cells)
    turned = jnp.transpose(jnp.concatenate([mine, pltpu.roll(mine, TILES, 1)], axis=0))
    loads = []
    for m in range(2):
        loads.append(
            jnp.concatenate(
                [turned[j * KD : (j + 1) * KD] * sights[m][j : j + 1, :] for j in range(CAP // 2)],
                axis=1,
            )
        )
    parts = dot(jnp.concatenate(split3(jnp.concatenate(loads, axis=0)), axis=0), one_hot, NT)
    n = 2 * KD
    return parts[0:n] + (parts[n : 2 * n] + parts[2 * n : 3 * n])


def copies_kernel(own, other, copies):
    copies[...] = jnp.broadcast_to((own[...] + other[...])[None], copies.shape)


def last_kernel(number, before, panel_high, panel_low, high, middle, low, spread_high, spread_low, matrix):
    matrix[...] = before[...]
    eliminate(matrix, number)
    inverse = matrix[...]
    high[...], middle[...], low[...] = split3(inverse)
    spread = dot3(split2(inverse), (panel_high[...], panel_low[...]), NN)
    spread_high[...], spread_low[...] = split2(spread)


def final_kernel(parts, high, middle, low, spread_high, spread_low, hessian, filtered, coefficients):
    a1, a2, a3 = split3(jnp.sum(parts[...], axis=0))
    removed = dot3((a1, a2), (spread_high[...], spread_low[...]), NN)
    b1, b2, b3 = high[...], middle[...], low[...]
    small = dot(a1, b3, NN) + dot(a3, b1, NN) + dot(a2, b2, NN)
    coefficients[...] = dot(a1, b1, NN) + ((dot(a1, b2, NN) + dot(a2, b1, NN)) + small)
    for x in range(CX):
        filtered[x] = hessian[x] - removed[:, x * NY : (x + 1) * NY]


def swap(value, axis, distance, offset=0):
    count = lax.axis_size(axis)
    partner = [((i + offset) ^ distance) - offset for i in range(count)]
    return lax.ppermute(value, axis, [(i, j) for i, j in enumerate(partner) if 0 <= j < count])


def per_device(
    probes, viscosity, friction, base_velocity, obs_tile, obs_cell, sight_lines, obs_precision, basis
):
    cells = CX * NY
    me = lax.axis_index("probe").astype(jnp.int32).reshape(1)
    at = lax.axis_index("tile").astype(jnp.int32).reshape(1)
    rows = obs_cell.shape[0]
    arguments = [
        viscosity.reshape(CX * NZ, NY),
        probes.reshape(CX * KD, NY),
        base_velocity.reshape(CX * 2, NY),
        friction,
        obs_tile.reshape(1, -1),
        obs_cell.reshape(1, -1),
        sight_lines,
    ]
    others = [swap(basis.reshape(-1, NY), "probe", d) for d in (1, 2, 3)]
    packed, edge_c, edge_d = call(
        prepare_kernel,
        [sds((PACK, NY)), sds((NZ, NY)), sds((NZ, NY))],
        [at, *arguments],
        places=[SM] + [pl.BlockSpec(memory_space=pltpu.HBM)] * len(arguments),
        scratch=[
            pltpu.VMEM((CX, NY), f32),
            pltpu.VMEM((1, rows), jnp.int32),
            pltpu.VMEM((1, rows), jnp.int32),
            pltpu.VMEM((2, rows), f32),
            pltpu.SemaphoreType.DMA((9,)),
        ],
        moved=400000,
        vmem=VMEM_PREP,
    )
    asked, slots, own_basis = call(
        meta_kernel,
        [sds((TILES, 128)), sds((2, rows), jnp.int32), sds((basis.shape[0] * CX, NY))],
        [packed, basis.reshape(-1, NY)],
        flops=10**10,
        moved=400000,
    )
    swap_a = swap(packed, "tile", 1)
    swap_b = swap(packed, "tile", 1, 1)
    far_c = swap(edge_c, "tile", 2)
    far_d = swap(edge_d, "tile", 2, 2)
    asked, swap_b, far_c, far_d = lax.optimization_barrier((asked, swap_b, far_c, far_d))
    n_basis = 4 * basis.shape[0]
    panel_high, panel_low, request = call(
        gram_kernel,
        [sds((n_basis, cells), bf16), sds((n_basis, cells), bf16), sds((TILES, 8, 128))],
        [me, own_basis, *others, asked],
        scratch=[pltpu.VMEM((HALF, HALF), f32)] * 3,
        scalars=1,
        flops=20 * 10**9,
        moved=1500000,
    )

    def exchange(value):
        return lax.all_to_all(value, "tile", split_axis=0, concat_axis=0, tiled=True)

    meta = exchange(request)
    precision_parts = call(
        split_kernel,
        [sds(obs_precision.shape, bf16), sds(obs_precision.shape, bf16)],
        [obs_precision],
        flops=2 * 10**9,
        moved=2000000,
    )
    precision_parts, meta = lax.optimization_barrier((precision_parts, meta))

    field = pltpu.VMEM((ROWS, 2, NZ, KD, NY), f32)
    load = pltpu.VMEM((ROWS, 2, KD, NY), f32)
    surface, coef, gain = call(
        state_kernel,
        [sds((2, CX, KD, NY)), sds((N_COEF, ROWS, NZ, NY)), sds((2, CX, NY))],
        [at, packed, swap_a, swap_b, far_c, far_d],
        scalars=1,
        scratch=[
            pltpu.VMEM((ROWS + 2, NZ, NY), f32),
            pltpu.VMEM((ROWS, NZ, NY), f32),
            pltpu.VMEM((ROWS, 1, NY), f32),
            load,
            field,
            field,
        ],
        flops=40 * 16 * 44 * 1024,
        moved=2000000,
    )
    payload = call(
        gather_kernel,
        sds((TILES, 8, 128)),
        [meta, surface],
        flops=2 * 48 * 512 * 1024,
        moved=300000,
    )
    arrived = exchange(payload)
    outgoing = call(
        precision_kernel,
        sds((TILES * 4, 128)),
        [arrived, slots, *precision_parts],
        flops=20 * 10**9,
        moved=1500000,
    )
    returned = exchange(outgoing.reshape(TILES, 4, 128)).reshape(TILES * 4, 128)
    matrix = call(
        first_kernel,
        sds((n_basis, n_basis)),
        [arrived],
        scratch=[pltpu.VMEM((HALF, HALF), f32)] * 3,
        flops=12 * 64 * 256 * 256,
        moved=500000,
    )
    number = 1

    def invert(matrix, pieces):
        nonlocal number
        for _ in range(pieces):
            matrix = call(
                functools.partial(next_kernel, number),
                sds((n_basis, n_basis)),
                [matrix],
                flops=12 * 64 * 256 * 256,
                moved=500000,
            )
            number += 1
        return matrix

    matrix = invert(matrix, PIECES[0])
    returned, matrix = lax.optimization_barrier((returned, matrix))
    hessian, moments = call(
        adjoint_kernel,
        [sds((CX, KD, NY)), sds((KD, n_basis))],
        [returned, meta, coef, gain, panel_high, panel_low],
        scratch=[load, field, field],
        flops=40 * 16 * 44 * 1024,
        moved=2000000,
    )
    moments, matrix = lax.optimization_barrier((moments, matrix))
    half = TILES // 2
    copies = call(
        copies_kernel,
        sds((half, KD, n_basis)),
        [moments, swap(moments, "tile", 1)],
        flops=half * KD * n_basis,
        moved=4 * half * KD * n_basis,
    )
    parts = lax.all_to_all(
        copies,
        "tile",
        split_axis=0,
        concat_axis=0,
        tiled=True,
        axis_index_groups=[list(range(core, TILES, 2)) for core in range(2)],
    )
    matrix = invert(matrix, PIECES[1])
    inverse = call(
        functools.partial(last_kernel, number),
        [sds((n_basis, n_basis), bf16)] * 3 + [sds((n_basis, cells), bf16)] * 2,
        [matrix, panel_high, panel_low],
        scratch=[pltpu.VMEM((n_basis, n_basis), f32)],
        flops=12 * 64 * 256 * 256 + 6 * 256 * 256 * 512,
        moved=1500000,
    )
    filtered, coefficients = call(
        final_kernel,
        [sds((CX, KD, NY)), sds((KD, n_basis))],
        [parts, *inverse, hessian],
        flops=12 * 8 * 256 * 512,
        moved=800000,
    )
    return filtered, coefficients


def solution(mesh):
    in_specs = (
        P("tile", "probe", None),
        P("tile", None, None),
        P("tile", None),
        P("tile", None, None),
        P("tile", None),
        P("tile"),
        P(None, "tile"),
        P("tile", None),
        P("probe", "tile", None),
    )
    out_specs = (P("tile", "probe", None), P("probe", None))
    return jax.shard_map(
        per_device, mesh=mesh, in_specs=in_specs, out_specs=out_specs, check_vma=False
    )
```

```python
import functools

import jax
import jax.numpy as jnp
from jax import lax
from jax.experimental import pallas as pl
from jax.experimental.pallas import tpu as pltpu
from jax.sharding import PartitionSpec as P

SWEEPS = 5
CX = 4
NY = 128
NZ = 16
KD = 8
CAP = 16
HALF = 128
TILES = 64
ROWS = CX * 3
ASPECT = 1024.0
N_COEF = 13
F_E, F_W, A_N, A_S, C_PP, C_MP, C_PM, C_MM, LOW, INV_U, INV_V, Q_U, Q_V = range(N_COEF)
BLOCK = 32
VMEM_PREP = 60
PIVOTS = 4
PIECES = (3, 3)
V_AT, P_AT, B_AT, F_AT = 0, CX * NZ, CX * (NZ + KD), CX * (NZ + KD + 2)
O_AT, PACK = F_AT + 4, F_AT + 24
f32 = jnp.float32
bf16 = jnp.bfloat16
VM = pl.BlockSpec(memory_space=pltpu.VMEM)
SM = pl.BlockSpec(memory_space=pltpu.SMEM)

NN = (((1,), (0,)), ((), ()))
NT = (((1,), (1,)), ((), ()))


def call(kernel, out_shape, args, scratch=(), scalars=0, flops=0, moved=0, places=None, vmem=14):
    single = not isinstance(out_shape, (list, tuple))
    shapes = [out_shape] if single else list(out_shape)
    out = pl.pallas_call(
        kernel,
        out_shape=shapes,
        in_specs=places or [SM] * scalars + [VM] * (len(args) - scalars),
        out_specs=[VM] * len(shapes),
        scratch_shapes=list(scratch),
        compiler_params=pltpu.CompilerParams(vmem_limit_bytes=int(vmem * 2**20)),
        cost_estimate=pl.CostEstimate(flops=flops, bytes_accessed=moved, transcendentals=0),
    )(*args)
    return out[0] if single else out


def sds(shape, dtype=f32):
    return jax.ShapeDtypeStruct(shape, dtype)


def dot(a, b, dims):
    return lax.dot_general(a, b, dims, preferred_element_type=f32)


def split2(x):
    high = x.astype(bf16)
    return high, (x - high.astype(f32)).astype(bf16)


def split3(x):
    high = x.astype(bf16)
    rest = x - high.astype(f32)
    middle = rest.astype(bf16)
    return high, middle, (rest - middle.astype(f32)).astype(bf16)


def dot3(a, b, dims):
    a_high, a_low = a
    b_high, b_low = b
    return dot(a_high, b_high, dims) + (dot(a_high, b_low, dims) + dot(a_low, b_high, dims))


def iota(shape, axis):
    return lax.broadcasted_iota(jnp.int32, shape, axis)


def prepare_kernel(
    at_ref, visc, probes, base, fric, tile_row, cell_row, sight,
    packed, edge_c, edge_d, fric_in, tile_in, cell_in, sight_in, sems,
):
    upper_pair = lax.rem(at_ref[0], 4) // 2
    high_row = pl.multiple_of((CX - 1) * NZ * (1 - upper_pair), NZ)
    low_row = pl.multiple_of((CX - 1) * NZ * upper_pair, NZ)
    moves = [
        (fric, fric_in),
        (tile_row, tile_in),
        (cell_row, cell_in),
        (sight, sight_in),
        (visc, packed.at[pl.ds(V_AT, CX * NZ), :]),
        (probes, packed.at[pl.ds(P_AT, CX * KD), :]),
        (base, packed.at[pl.ds(B_AT, CX * 2), :]),
        (visc.at[pl.ds(high_row, NZ), :], edge_c),
        (visc.at[pl.ds(low_row, NZ), :], edge_d),
    ]
    copies = [
        pltpu.make_async_copy(source, target, sems.at[n])
        for n, (source, target) in enumerate(moves)
    ]
    for copy in copies:
        copy.start()
    for copy in copies:
        copy.wait()
    tail = [fric_in[...]]
    for line in (tile_in[...], cell_in[...], sight_in[0:1, :], sight_in[1:2, :]):
        tail += [line[:, n : n + 128].astype(f32) for n in range(0, line.shape[1], 128)]
    tail.append(jnp.zeros((4, NY), f32))
    packed[F_AT:PACK, :] = jnp.concatenate(tail, axis=0)


def meta_kernel(packed, basis, asked, slots, own_basis):
    own_basis[...] = basis[...]
    rows = slots.shape[1]

    def line(at):
        start = O_AT + at * (rows // 128)
        return jnp.concatenate(
            [packed[n : n + 1, :] for n in range(start, start + rows // 128)], axis=1
        )

    tiles = line(0).astype(jnp.int32)
    one_hot = (iota((TILES, rows), 0) == tiles).astype(f32)
    before = (iota((rows, rows), 0) < iota((rows, rows), 1)).astype(f32).astype(bf16)
    one_hot_b = one_hot.astype(bf16)
    earlier = dot(one_hot_b, before, NN)
    rank = jnp.sum(one_hot * earlier, axis=0, keepdims=True).astype(jnp.int32)
    slots[0:1, :] = tiles
    slots[1:2, :] = rank
    chosen = (iota((CAP, rows), 0) == rank).astype(f32)
    values = jnp.concatenate(
        [
            chosen * line(1),
            chosen * line(2),
            chosen * line(3),
            jnp.zeros((128 - 3 * CAP, rows), f32),
        ],
        axis=0,
    )
    parts = [dot(one_hot_b, part, NT) for part in split3(values)]
    asked[...] = parts[0] + (parts[1] + parts[2])


def build_coefs(visc, fric, coef, upper):
    lane = iota((NZ, NY), 1)
    layer = iota((NZ, NY), 0)

    def row(i, carry):
        centre = visc[i]
        east = visc[i + 1]
        west = visc[i - 1]

        def from_south(x):
            return pltpu.roll(x, 1, 1)

        def from_north(x):
            return pltpu.roll(x, NY - 1, 1)

        south_centre = jnp.where(lane == 0, 0.0, from_south(centre))
        north_centre = jnp.where(lane == NY - 1, 0.0, from_north(centre))
        face_e = 0.5 * (centre + east)
        face_w = 0.5 * (centre + west)
        face_n = 0.5 * (centre + north_centre)
        face_s = 0.5 * (centre + south_centre)
        coef[F_E, i - 1] = face_e
        coef[F_W, i - 1] = face_w
        coef[A_N, i - 1] = jnp.where(lane == 0, 0.0, face_s)
        coef[A_S, i - 1] = jnp.where(lane == NY - 1, 0.0, face_n)
        coef[C_PP, i - 1] = jnp.where(lane == 0, 0.0, 0.375 * (south_centre + east))
        coef[C_MP, i - 1] = jnp.where(lane == 0, 0.0, -0.375 * (south_centre + west))
        coef[C_PM, i - 1] = jnp.where(lane == NY - 1, 0.0, -0.375 * (north_centre + east))
        coef[C_MM, i - 1] = jnp.where(lane == NY - 1, 0.0, 0.375 * (north_centre + west))
        above = pltpu.roll(centre, NZ - 1, 0)
        up = jnp.where(layer == NZ - 1, 0.0, ASPECT * 0.5 * (centre + above))
        down = jnp.where(layer == 0, 0.0, pltpu.roll(up, 1, 0))
        coef[LOW, i - 1] = down
        upper[i - 1] = up
        column = (up + down) + jnp.where(layer == 0, fric[i - 1], 0.0)
        coef[INV_U, i - 1] = 4.0 * (face_e + face_w) + (face_n + face_s) + column
        coef[INV_V, i - 1] = face_e + face_w + 4.0 * (face_n + face_s) + column
        return carry

    lax.fori_loop(1, ROWS + 1, row, 0)
    inside = visc[pl.ds(1, ROWS), 0, :] > 0.0
    ratio_u = ratio_v = None
    for layer_index in range(NZ):
        pivot_u = coef[INV_U, :, layer_index, :]
        pivot_v = coef[INV_V, :, layer_index, :]
        if layer_index > 0:
            low = coef[LOW, :, layer_index, :]
            pivot_u = pivot_u - low * ratio_u
            pivot_v = pivot_v - low * ratio_v
        inverse_u = jnp.where(inside, 1.0 / pivot_u, 0.0)
        inverse_v = jnp.where(inside, 1.0 / pivot_v, 0.0)
        up = upper[:, layer_index, :]
        ratio_u = up * inverse_u
        ratio_v = up * inverse_v
        coef[INV_U, :, layer_index, :] = inverse_u
        coef[INV_V, :, layer_index, :] = inverse_v
        coef[Q_U, :, layer_index, :] = ratio_u
        coef[Q_V, :, layer_index, :] = ratio_v


def run_sweeps(coef, load, fields, load_layer, finish):
    far = NZ - 1 if load_layer == 0 else 0

    def take(which, i, layer_index):
        return jnp.broadcast_to(coef[which, i, layer_index : layer_index + 1, :], (KD, NY))

    def solve(i, right_u, right_v, last):
        forward_u, forward_v = [], []
        for k in range(NZ):
            u, v = right_u(k), right_v(k)
            if k == load_layer:
                u = load[i, 0] if u is None else u + load[i, 0]
                v = load[i, 1] if v is None else v + load[i, 1]
            if k > 0 and forward_u[-1] is not None:
                low = take(LOW, i, k)
                below_u, below_v = low * forward_u[-1], low * forward_v[-1]
                u = below_u if u is None else u + below_u
                v = below_v if v is None else v + below_v
            forward_u.append(None if u is None else u * take(INV_U, i, k))
            forward_v.append(None if v is None else v * take(INV_V, i, k))
        solved_u, solved_v = [None] * NZ, [None] * NZ
        solved_u[-1], solved_v[-1] = forward_u[-1], forward_v[-1]
        if not (last and far == NZ - 1):
            for k in range(NZ - 2, -1, -1):
                u = take(Q_U, i, k) * solved_u[k + 1]
                v = take(Q_V, i, k) * solved_v[k + 1]
                solved_u[k] = u if forward_u[k] is None else forward_u[k] + u
                solved_v[k] = v if forward_v[k] is None else forward_v[k] + v
        return solved_u, solved_v

    for sweep in range(SWEEPS):
        source, target = fields[(sweep + 1) % 2], fields[sweep % 2]
        last = sweep == SWEEPS - 1

        def row(i, carry, sweep=sweep, source=source, target=target, last=last):
            if sweep == 0:
                nothing = lambda k: None
                solved_u, solved_v = solve(i, nothing, nothing, last)
            else:

                def sides(component, k, along):
                    other = 1 - component
                    mine, east, west = (source[i + d, component, k] for d in (0, 1, -1))
                    cross_e, cross_w = (source[i + d, other, k] for d in (1, -1))
                    direct = take(F_E, i, k) * east + take(F_W, i, k) * west
                    if along:
                        direct = 4.0 * direct
                        scaled = mine
                    else:
                        scaled = 4.0 * mine
                    north = take(A_N, i, k) * scaled + (
                        take(C_PP, i, k) * cross_e + take(C_MP, i, k) * cross_w
                    )
                    south = take(A_S, i, k) * scaled + (
                        take(C_PM, i, k) * cross_e + take(C_MM, i, k) * cross_w
                    )
                    return direct + (pltpu.roll(north, NY - 1, 1) + pltpu.roll(south, 1, 1))

                solved_u, solved_v = solve(
                    i,
                    lambda k: sides(0, k, True),
                    lambda k: sides(1, k, False),
                    last,
                )
            if last:
                finish(i - CX, solved_u[far], solved_v[far])
            else:
                for k in range(NZ):
                    target[i, 0, k] = solved_u[k]
                    target[i, 1, k] = solved_v[k]
            return carry

        def pair(j, carry, row=row, sweep=sweep):
            return row(sweep + 2 * j + 1, row(sweep + 2 * j, carry))

        lax.fori_loop(0, ROWS // 2 - sweep, pair, 0)


def sides_of(at):
    odd = lax.rem(at, 2)
    return 2 - 2 * odd, 2 * odd


def state_kernel(
    at_ref, own, swap_a, swap_b, edge_c, edge_d, surface, coef, gain, visc, upper, fric, load, field_a, field_b
):
    at = at_ref[0]
    part_a, part_b = sides_of(at)
    upper_pair = lax.rem(at, 4) // 2
    visc[(ROWS + 1) * (1 - upper_pair)] = edge_c[...]
    visc[(ROWS + 1) * upper_pair] = edge_d[...]
    for part, packed in ((part_a, swap_a), (1, own), (part_b, swap_b)):
        for x in range(CX):
            i = part * CX + x
            visc[i + 1] = packed[V_AT + x * NZ : V_AT + (x + 1) * NZ, :]
            friction = packed[F_AT + x : F_AT + x + 1, :]
            fric[i] = friction
            probes = packed[P_AT + x * KD : P_AT + (x + 1) * KD, :]
            for m in range(2):
                basal = -(friction * packed[B_AT + 2 * x + m : B_AT + 2 * x + m + 1, :])
                if packed is own:
                    gain[m, x : x + 1, :] = basal
                load[i, m] = basal * probes
    build_coefs(visc, fric, coef, upper)

    def finish(x, u, v):
        surface[0, x] = u
        surface[1, x] = v

    run_sweeps(coef, load, (field_a, field_b), 0, finish)


def adjoint_kernel(
    returned, meta, coef, gain, panel_high, panel_low, hessian, moments, load, field_a, field_b
):
    beside = meta[:, 1, :]
    metas = (beside, meta[:, 0, :], pltpu.roll(beside, TILES, 1))
    for part, k in enumerate((1, 0, 2)):
        top = top_load(returned[pl.ds(k, TILES, stride=4), :], metas[part])
        for x in range(CX):
            for m in range(2):
                load[part * CX + x, m] = top[m * KD : (m + 1) * KD, x * NY : (x + 1) * NY]

    def finish(x, u, v):
        hessian[x] = gain[0, pl.ds(x, 1), :] * u + gain[1, pl.ds(x, 1), :] * v

    run_sweeps(coef, load, (field_a, field_b), NZ - 1, finish)
    whole = jnp.concatenate([hessian[x] for x in range(CX)], axis=1)
    moments[...] = dot3(split2(whole), (panel_high[...], panel_low[...]), NT)


def from_tile(value, shift):
    moved = pltpu.roll(value, -shift % TILES, 0)
    edge = TILES - 1 if shift > 0 else 0
    return jnp.where(iota(value.shape, 0) == edge, 0.0, moved)


def gram_kernel(
    me_ref, own, near, across, back, asked, panel_high, panel_low, payload, gram_11, gram_12, gram_22
):
    me = me_ref[0]
    count = own.shape[0] // CX
    for shift, block in enumerate((own, near, across, back)):
        source = me ^ shift
        flat = jnp.concatenate(
            [block[pl.ds(x, count, stride=CX), :] for x in range(CX)], axis=1
        )
        at = pl.ds(pl.multiple_of(source * count, count), count)
        panel_high[at, :], panel_low[at, :] = split2(flat)
    upper = panel_high[0:HALF, :], panel_low[0:HALF, :]
    lower = panel_high[HALF:, :], panel_low[HALF:, :]
    gram_11[...] = dot3(upper, upper, NT)
    gram_12[...] = dot3(upper, lower, NT)
    gram_22[...] = dot3(lower, lower, NT)
    here = asked[...]
    payload[:, 0, :] = here
    payload[:, 1, :] = from_tile(here, -1) + pltpu.roll(from_tile(here, 1), TILES, 1)
    for k, n, block in gram_lines(gram_11, gram_12, gram_22):
        payload[:, k, :] = block[pl.ds(n, TILES, stride=2), :]


def gram_lines(gram_11, gram_12, gram_22):
    return (2, 0, gram_11), (3, 0, gram_12), (4, 1, gram_11), (5, 1, gram_12), (6, 0, gram_22), (7, 1, gram_22)


def small_inverse(p):
    size = len(p)
    if size == 2:
        (a, b), (_, d) = p
        scale = 1.0 / (a * d - b * b)
        off = -b * scale
        return [[d * scale, off], [off, a * scale]]
    h = size // 2

    def times(x, y):
        return [
            [functools.reduce(lambda u, v: u + v, [x[i][k] * y[k][j] for k in range(h)]) for j in range(h)]
            for i in range(h)
        ]

    a = [row[:h] for row in p[:h]]
    b = [row[h:] for row in p[:h]]
    c = [row[:h] for row in p[h:]]
    d = [row[h:] for row in p[h:]]
    a_inv = small_inverse(a)
    x = times(a_inv, b)
    cx = times(c, x)
    s_inv = small_inverse([[d[i][j] - cx[i][j] for j in range(h)] for i in range(h)])
    xs = times(x, s_inv)
    x_t = [[x[j][i] for j in range(h)] for i in range(h)]
    corner = times(xs, x_t)
    top = [
        [a_inv[i][j] + corner[i][j] for j in range(h)] + [-xs[i][j] for j in range(h)]
        for i in range(h)
    ]
    bottom = [[-xs[j][i] for j in range(h)] + s_inv[i] for i in range(h)]
    return top + bottom


def invert_block(block):
    size = block.shape[0]
    row_of = iota(block.shape, 0)
    lane_of = iota(block.shape, 1)
    for k in range(0, size, PIVOTS):
        columns = [jnp.broadcast_to(block[:, k + j : k + j + 1], block.shape) for j in range(PIVOTS)]
        pivots = [[columns[j][k + i : k + i + 1, :] for j in range(PIVOTS)] for i in range(PIVOTS)]
        inverse = small_inverse(pivots)
        own_lane = (lane_of >= k) & (lane_of < k + PIVOTS)
        own = own_lane | ((row_of >= k) & (row_of < k + PIVOTS))
        rows = [
            jnp.where(
                own_lane[0:1, :],
                jnp.where(lane_of[0:1, :] == k + j, 1.0, 0.0),
                block[k + j : k + j + 1, :],
            )
            for j in range(PIVOTS)
        ]
        block = jnp.where(own, 0.0, block)
        in_rows = (row_of >= k) & (row_of < k + PIVOTS)
        for j in range(PIVOTS):
            row = functools.reduce(
                lambda u, v: u + v, [inverse[j][i] * rows[i] for i in range(PIVOTS)]
            )
            column = jnp.where(in_rows, jnp.where(row_of == k + j, -1.0, 0.0), columns[j])
            block = block - column * row
    return block


def dot_f32(a, b):
    a1, a2, a3 = split3(a)
    b1, b2, b3 = split3(b)
    small = dot(a1, b3, NN) + dot(a3, b1, NN) + dot(a2, b2, NN)
    return dot(a1, b1, NN) + ((dot(a1, b2, NN) + dot(a2, b1, NN)) + small)


def eliminate(matrix, number):
    size = matrix.shape[0]
    at = slice(number * BLOCK, (number + 1) * BLOCK)
    inverse = invert_block(matrix[at, at])
    panel = matrix[at, :]
    columns = matrix[:, at]
    lanes = iota((BLOCK, size), 1)
    own_lanes = (lanes >= number * BLOCK) & (lanes < (number + 1) * BLOCK)
    identity = (iota((BLOCK, size), 0) + number * BLOCK == lanes).astype(f32)
    rows = dot_f32(inverse, jnp.where(own_lanes, identity, panel))
    rest = matrix[...]
    all_lanes = iota((size, size), 1)
    inside = (all_lanes >= number * BLOCK) & (all_lanes < (number + 1) * BLOCK)
    matrix[...] = jnp.where(inside, 0.0, rest) - dot_f32(columns, rows)
    matrix[at, :] = rows


def first_kernel(arrived, matrix, gram_11, gram_12, gram_22):
    for k, n, block in gram_lines(gram_11, gram_12, gram_22):
        block[pl.ds(n, TILES, stride=2), :] = arrived[:, k, :]
    matrix[0:HALF, 0:HALF] = gram_11[...]
    matrix[0:HALF, HALF:] = gram_12[...]
    matrix[HALF:, 0:HALF] = jnp.transpose(gram_12[...])
    matrix[HALF:, HALF:] = gram_22[...]
    eliminate(matrix, 0)


def next_kernel(number, before, matrix):
    matrix[...] = before[...]
    eliminate(matrix, number)


def slot_rows(meta):
    wide = jnp.concatenate([meta, jnp.zeros((128 - TILES, 128), f32)], axis=0)
    turned = jnp.transpose(wide)
    half = CAP // 2

    def paired(at):
        return turned[at : at + half] + pltpu.roll(turned[at + half : at + CAP], TILES, 1)

    return paired(0), paired(CAP), paired(2 * CAP)


def slot_one_hot(cells):
    index = cells.astype(jnp.int32)
    at = iota((CX * NY, 128), 0)
    return jnp.concatenate(
        [(at == index[j : j + 1, :]).astype(f32).astype(bf16) for j in range(CAP // 2)], axis=1
    )


def gather_kernel(meta, surface, payload):
    cells, sight_u, sight_v = slot_rows(meta[:, 0, :])
    one_hot = slot_one_hot(cells)
    both = jnp.concatenate(
        [jnp.concatenate([surface[m, x] for x in range(CX)], axis=1) for m in range(2)], axis=0
    )
    picked = dot(jnp.concatenate(split3(both), axis=0), one_hot, NN)
    n = 2 * KD
    picked = picked[0:n] + (picked[n : 2 * n] + picked[2 * n : 3 * n])
    chunks = []
    for j in range(CAP // 2):
        at = slice(j * 128, (j + 1) * 128)
        chunks.append(
            sight_u[j : j + 1, :] * picked[0:KD, at] + sight_v[j : j + 1, :] * picked[KD:n, at]
        )
    chunks.append(jnp.zeros((128 - TILES, 128), f32))
    turned = jnp.transpose(jnp.concatenate(chunks, axis=0))
    payload[...] = jnp.broadcast_to(jnp.sum(meta[...], axis=0, keepdims=True), payload.shape)
    payload[:, 0, :] = turned[0:TILES] + pltpu.roll(turned[TILES:], TILES, 1)


def split_kernel(precision, high, low):
    high[...], low[...] = split2(precision[...])


def precision_kernel(arrived, slots, precision_high, precision_low, payload):
    rows = precision_high.shape[0]

    one_hot = (iota((128, rows), 0) == slots[0:1, :]).astype(f32).astype(bf16)
    rank = slots[1:2, :]
    mine = arrived[:, 0, :]
    turned = jnp.transpose(jnp.concatenate([mine, jnp.zeros((128 - TILES, 128), f32)], axis=0))
    spread = [dot(part, one_hot, NN) for part in split3(turned)]
    spread = spread[0] + (spread[1] + spread[2])
    predicted = jnp.zeros((KD, rows), f32)
    for s in range(CAP):
        predicted = predicted + jnp.where(rank == s, spread[s * KD : (s + 1) * KD], 0.0)
    weighted = dot3(split2(predicted), (precision_high[...], precision_low[...]), NN)
    spots = jnp.concatenate([jnp.where(rank == s, weighted, 0.0) for s in range(CAP)], axis=0)
    sent = [dot(one_hot, part, NT) for part in split3(spots)]
    sent = sent[0] + (sent[1] + sent[2])
    sent = sent[0:TILES]
    payload[pl.ds(0, TILES, stride=4), :] = sent
    payload[pl.ds(1, TILES, stride=4), :] = from_tile(sent, -1)
    payload[pl.ds(2, TILES, stride=4), :] = from_tile(sent, 1)
    payload[pl.ds(3, TILES, stride=4), :] = jnp.zeros((TILES, 128), f32)


def top_load(mine, meta):
    cells, *sights = slot_rows(meta)
    one_hot = slot_one_hot(cells)
    turned = jnp.transpose(jnp.concatenate([mine, pltpu.roll(mine, TILES, 1)], axis=0))
    loads = []
    for m in range(2):
        loads.append(
            jnp.concatenate(
                [turned[j * KD : (j + 1) * KD] * sights[m][j : j + 1, :] for j in range(CAP // 2)],
                axis=1,
            )
        )
    parts = dot(jnp.concatenate(split3(jnp.concatenate(loads, axis=0)), axis=0), one_hot, NT)
    n = 2 * KD
    return parts[0:n] + (parts[n : 2 * n] + parts[2 * n : 3 * n])


def copies_kernel(own, other, copies):
    copies[...] = jnp.broadcast_to((own[...] + other[...])[None], copies.shape)


def last_kernel(number, before, panel_high, panel_low, high, middle, low, spread_high, spread_low, matrix):
    matrix[...] = before[...]
    eliminate(matrix, number)
    inverse = matrix[...]
    high[...], middle[...], low[...] = split3(inverse)
    spread = dot3(split2(inverse), (panel_high[...], panel_low[...]), NN)
    spread_high[...], spread_low[...] = split2(spread)


def final_kernel(parts, high, middle, low, spread_high, spread_low, hessian, filtered, coefficients):
    a1, a2, a3 = split3(jnp.sum(parts[...], axis=0))
    removed = dot3((a1, a2), (spread_high[...], spread_low[...]), NN)
    b1, b2, b3 = high[...], middle[...], low[...]
    small = dot(a1, b3, NN) + dot(a3, b1, NN) + dot(a2, b2, NN)
    coefficients[...] = dot(a1, b1, NN) + ((dot(a1, b2, NN) + dot(a2, b1, NN)) + small)
    for x in range(CX):
        filtered[x] = hessian[x] - removed[:, x * NY : (x + 1) * NY]


def swap(value, axis, distance, offset=0):
    count = lax.axis_size(axis)
    partner = [((i + offset) ^ distance) - offset for i in range(count)]
    return lax.ppermute(value, axis, [(i, j) for i, j in enumerate(partner) if 0 <= j < count])


def per_device(
    probes, viscosity, friction, base_velocity, obs_tile, obs_cell, sight_lines, obs_precision, basis
):
    cells = CX * NY
    me = lax.axis_index("probe").astype(jnp.int32).reshape(1)
    at = lax.axis_index("tile").astype(jnp.int32).reshape(1)
    rows = obs_cell.shape[0]
    arguments = [
        viscosity.reshape(CX * NZ, NY),
        probes.reshape(CX * KD, NY),
        base_velocity.reshape(CX * 2, NY),
        friction,
        obs_tile.reshape(1, -1),
        obs_cell.reshape(1, -1),
        sight_lines,
    ]
    others = [swap(basis.reshape(-1, NY), "probe", d) for d in (1, 2, 3)]
    packed, edge_c, edge_d = call(
        prepare_kernel,
        [sds((PACK, NY)), sds((NZ, NY)), sds((NZ, NY))],
        [at, *arguments],
        places=[SM] + [pl.BlockSpec(memory_space=pltpu.HBM)] * len(arguments),
        scratch=[
            pltpu.VMEM((CX, NY), f32),
            pltpu.VMEM((1, rows), jnp.int32),
            pltpu.VMEM((1, rows), jnp.int32),
            pltpu.VMEM((2, rows), f32),
            pltpu.SemaphoreType.DMA((9,)),
        ],
        moved=400000,
        vmem=VMEM_PREP,
    )
    asked, slots, own_basis = call(
        meta_kernel,
        [sds((TILES, 128)), sds((2, rows), jnp.int32), sds((basis.shape[0] * CX, NY))],
        [packed, basis.reshape(-1, NY)],
        flops=10**10,
        moved=400000,
    )
    swap_a = swap(packed, "tile", 1)
    swap_b = swap(packed, "tile", 1, 1)
    far_c = swap(edge_c, "tile", 2)
    far_d = swap(edge_d, "tile", 2, 2)
    asked, swap_b, far_d = lax.optimization_barrier((asked, swap_b, far_d))
    n_basis = 4 * basis.shape[0]
    panel_high, panel_low, request = call(
        gram_kernel,
        [sds((n_basis, cells), bf16), sds((n_basis, cells), bf16), sds((TILES, 8, 128))],
        [me, own_basis, *others, asked],
        scratch=[pltpu.VMEM((HALF, HALF), f32)] * 3,
        scalars=1,
        flops=20 * 10**9,
        moved=1500000,
    )

    def exchange(value):
        return lax.all_to_all(value, "tile", split_axis=0, concat_axis=0, tiled=True)

    meta = exchange(request)
    precision_parts = call(
        split_kernel,
        [sds(obs_precision.shape, bf16), sds(obs_precision.shape, bf16)],
        [obs_precision],
        flops=2 * 10**9,
        moved=2000000,
    )
    precision_parts, meta = lax.optimization_barrier((precision_parts, meta))

    field = pltpu.VMEM((ROWS, 2, NZ, KD, NY), f32)
    load = pltpu.VMEM((ROWS, 2, KD, NY), f32)
    surface, coef, gain = call(
        state_kernel,
        [sds((2, CX, KD, NY)), sds((N_COEF, ROWS, NZ, NY)), sds((2, CX, NY))],
        [at, packed, swap_a, swap_b, far_c, far_d],
        scalars=1,
        scratch=[
            pltpu.VMEM((ROWS + 2, NZ, NY), f32),
            pltpu.VMEM((ROWS, NZ, NY), f32),
            pltpu.VMEM((ROWS, 1, NY), f32),
            load,
            field,
            field,
        ],
        flops=40 * 16 * 44 * 1024,
        moved=2000000,
    )
    payload = call(
        gather_kernel,
        sds((TILES, 8, 128)),
        [meta, surface],
        flops=2 * 48 * 512 * 1024,
        moved=300000,
    )
    arrived = exchange(payload)
    outgoing = call(
        precision_kernel,
        sds((TILES * 4, 128)),
        [arrived, slots, *precision_parts],
        flops=20 * 10**9,
        moved=1500000,
    )
    returned = exchange(outgoing.reshape(TILES, 4, 128)).reshape(TILES * 4, 128)
    matrix = call(
        first_kernel,
        sds((n_basis, n_basis)),
        [arrived],
        scratch=[pltpu.VMEM((HALF, HALF), f32)] * 3,
        flops=12 * 64 * 256 * 256,
        moved=500000,
    )
    number = 1

    def invert(matrix, pieces):
        nonlocal number
        for _ in range(pieces):
            matrix = call(
                functools.partial(next_kernel, number),
                sds((n_basis, n_basis)),
                [matrix],
                flops=12 * 64 * 256 * 256,
                moved=500000,
            )
            number += 1
        return matrix

    matrix = invert(matrix, PIECES[0])
    returned, matrix = lax.optimization_barrier((returned, matrix))
    hessian, moments = call(
        adjoint_kernel,
        [sds((CX, KD, NY)), sds((KD, n_basis))],
        [returned, meta, coef, gain, panel_high, panel_low],
        scratch=[load, field, field],
        flops=40 * 16 * 44 * 1024,
        moved=2000000,
    )
    moments, matrix = lax.optimization_barrier((moments, matrix))
    half = TILES // 2
    copies = call(
        copies_kernel,
        sds((half, KD, n_basis)),
        [moments, swap(moments, "tile", 1)],
        flops=half * KD * n_basis,
        moved=4 * half * KD * n_basis,
    )
    parts = lax.all_to_all(
        copies,
        "tile",
        split_axis=0,
        concat_axis=0,
        tiled=True,
        axis_index_groups=[list(range(core, TILES, 2)) for core in range(2)],
    )
    matrix = invert(matrix, PIECES[1])
    inverse = call(
        functools.partial(last_kernel, number),
        [sds((n_basis, n_basis), bf16)] * 3 + [sds((n_basis, cells), bf16)] * 2,
        [matrix, panel_high, panel_low],
        scratch=[pltpu.VMEM((n_basis, n_basis), f32)],
        flops=12 * 64 * 256 * 256 + 6 * 256 * 256 * 512,
        moved=1500000,
    )
    filtered, coefficients = call(
        final_kernel,
        [sds((CX, KD, NY)), sds((KD, n_basis))],
        [parts, *inverse, hessian],
        flops=12 * 8 * 256 * 512,
        moved=800000,
    )
    return filtered, coefficients


def solution(mesh):
    in_specs = (
        P("tile", "probe", None),
        P("tile", None, None),
        P("tile", None),
        P("tile", None, None),
        P("tile", None),
        P("tile"),
        P(None, "tile"),
        P("tile", None),
        P("probe", "tile", None),
    )
    out_specs = (P("tile", "probe", None), P("probe", None))
    return jax.shard_map(
        per_device, mesh=mesh, in_specs=in_specs, out_specs=out_specs, check_vma=False
    )
```
